256 devices in a mesh: cluster: 16 (over z, core), sub: 16 (over y, x).
Axes of the slice: x: 4, y: 4, z: 8, core: 2. Of those that a mesh axis runs over, the one named last changes fastest.
Arguments:
- dual_ops: bfloat16 [16, 16, 2048, 2048], P('cluster', 'sub'), as said below
- local_load: float32 [16, 16, 2048, 128], P('cluster', 'sub'), may hold values from -6 to 6
- rigid_modes: float32 [16, 16, 6, 2048], P('cluster', 'sub'), may hold values from -0.044194174 to 0.044194174, as said below
- coarse_load: float32 [16, 6, 128], P('cluster'), may hold values from -6 to 6
- gluing_peer: int32 [16, 16, 16], P('cluster', 'sub'), may hold values from 0 to 3, as said below
- gluing_sign: int32 [16, 16, 16], P('cluster', 'sub'), may hold values from -1 to 1, as said below
Outputs:
- multipliers: float32 [16, 16, 2048, 128], P('cluster', 'sub')
- amplitudes: float32 [16, 6, 128], P('cluster')
The draws below stay inside these ranges and needn't reach their ends.
Inputs may be any that keep to these rules, and one draw needn't show every extreme that they name: `gluing_peer`: gluing is consistent: if block 4 k + f of subdomain t names peer j, the neighbour's block 4 j + (f xor 1) names k back; the map is one to one between facing blocks of two neighbours. Entries for missing neighbours are still in range. `gluing_sign`: every entry is -1 or 1; the two glued blocks of a neighbour pair carry opposite signs. `dual_ops`: each local dual operator is symmetric positive definite. `rigid_modes`: two glued blocks of neighbouring subdomains carry equal traces of every mode, entry by entry.
All inputs are finite; a program needn't handle non-finite values.
Results may differ from the reference program's by a relative error of at most 0.003.
Values sent between devices are 32-bit elements; how exact they have to be, the bound alone decides.
A program may use at most 64 MiB of HBM per device.

```python
import jax
import jax.numpy as jnp
from jax import lax

M = 2048
BLOCKS = 16
BLOCK = 128
MODES = 6
LOADS = 128
ITERS = 2
CLUSTERS = 16
SUBS = 16


def gluing_tables(key):
    key_first, key_second, key_third, key_fourth = jax.random.split(key, 4)

    def forward_map(key_part):
        scores = jax.random.randint(key_part, (CLUSTERS, SUBS, 4), 0, 1 << 20) * 4 + jnp.arange(4, dtype=jnp.int32)
        return jnp.argsort(scores, axis=-1, stable=True).astype(jnp.int32)

    def sign_draw(key_part):
        return (2 * jax.random.randint(key_part, (CLUSTERS, SUBS, 4), 0, 2) - 1).astype(jnp.int32)

    def backward_map(forward_table, sign_table, axis_id):
        inverse = jnp.argsort(forward_table, axis=-1, stable=True).astype(jnp.int32)
        prior_inverse = jnp.roll(inverse, 1, axis=axis_id)
        prior_sign = jnp.roll(sign_table, 1, axis=axis_id)
        return (prior_inverse, -jnp.take_along_axis(prior_sign, prior_inverse, axis=-1))
    forward_sub = forward_map(key_first)
    forward_cluster = forward_map(key_second)
    sign_sub = sign_draw(key_third)
    sign_cluster = sign_draw(key_fourth)
    back_sub, back_sub_sign = backward_map(forward_sub, sign_sub, 1)
    back_cluster, back_cluster_sign = backward_map(forward_cluster, sign_cluster, 0)
    peer_table = jnp.stack([back_sub, forward_sub, back_cluster, forward_cluster], axis=-1)
    sign_table = jnp.stack([back_sub_sign, sign_sub, back_cluster_sign, sign_cluster], axis=-1)
    return (peer_table.reshape(CLUSTERS, SUBS, BLOCKS).astype(jnp.int32), sign_table.reshape(CLUSTERS, SUBS, BLOCKS).astype(jnp.int32))


def draw_gluing_peer(key, part):
    return gluing_tables(key)[0]


def draw_gluing_sign(key, part):
    return gluing_tables(key)[1]


def draw_rigid_modes(key, part):
    peer_table = gluing_tables(key)[0].reshape(CLUSTERS, SUBS, 4, 4)
    key = jax.random.fold_in(key, 23)
    key_first, key_second = jax.random.split(key, 2)
    factor = (4.0 * BLOCK * SUBS) ** (-0.5)
    sub_edge = jax.random.truncated_normal(key_first, -4.0, 4.0, (CLUSTERS, SUBS, 4, MODES, BLOCK), jnp.float32) * factor
    cluster_edge = jax.random.truncated_normal(key_second, -4.0, 4.0, (CLUSTERS, SUBS, 4, MODES, BLOCK), jnp.float32) * factor

    def pick(edge, index):
        return jnp.take_along_axis(edge, index[:, :, :, None, None], axis=2)
    face_prev_sub = pick(jnp.roll(sub_edge, 1, axis=1), peer_table[:, :, :, 0])
    face_prev_cluster = pick(jnp.roll(cluster_edge, 1, axis=0), peer_table[:, :, :, 2])
    stacked = jnp.stack([face_prev_sub, sub_edge, face_prev_cluster, cluster_edge], axis=3)
    return jnp.transpose(stacked, (0, 1, 4, 2, 3, 5)).reshape(CLUSTERS, SUBS, MODES, M)


def draw_dual_ops(key, part):
    key = jax.random.fold_in(key, 11)
    key_first, key_second = jax.random.split(key, 2)
    uniform_part = jax.random.uniform(key_first, (CLUSTERS, SUBS, M, M), jnp.float32, -1.0, 1.0)
    coupling = (uniform_part + jnp.swapaxes(uniform_part, -1, -2)) * (0.55 / M ** 0.5)
    diagonal = jnp.exp(jax.random.uniform(key_second, (CLUSTERS, SUBS, M), jnp.float32, jnp.log(1.2), jnp.log(3.0)))
    identity = jnp.arange(M)[:, None] == jnp.arange(M)[None, :]
    matrix = jnp.where(identity, diagonal[..., :, None], coupling)
    return matrix.astype(jnp.bfloat16)


def levels(rng, extent, cuts, low, top_value):
    factor_of, own = 1.0, jax.random.fold_in(rng, 6)
    for axis_at, parts in cuts:
        steps = jnp.exp(jax.random.uniform(jax.random.fold_in(own, axis_at), (parts,), jnp.float32, low / len(cuts), top_value / len(cuts)))
        factor_of = factor_of * jnp.repeat(steps, extent[axis_at] // parts).reshape([-1 if axis == axis_at else 1 for axis in range(len(extent))])
    return factor_of


def normal_values(stream_key, extent, width, most, pieces=(), held_as=jnp.bfloat16):
    loudness = levels(stream_key, extent, pieces, -0.22, 0.18) if pieces else 1.0
    result = jax.random.normal(stream_key, extent, jnp.float32) * width * loudness
    return jnp.minimum(jnp.maximum(result, -most), most).astype(held_as)


def setup_inputs(seed: int = 0) -> dict:
    streams_of = jax.random.split(jax.random.key(seed), 7)
    return {
        "dual_ops": draw_dual_ops(jax.random.fold_in(streams_of[6], 71), 0),
        "local_load": normal_values(streams_of[1], (CLUSTERS, SUBS, M, LOADS), 1.0, 6.0, ((0, 16), (1, 16)), jnp.float32),
        "rigid_modes": draw_rigid_modes(jax.random.fold_in(streams_of[6], 71), 0),
        "coarse_load": normal_values(streams_of[3], (CLUSTERS, MODES, LOADS), 1.0, 6.0, ((0, 16),), jnp.float32),
        "gluing_peer": draw_gluing_peer(jax.random.fold_in(streams_of[6], 71), 0),
        "gluing_sign": draw_gluing_sign(jax.random.fold_in(streams_of[6], 71), 0),
    }


HIGHEST = lax.Precision.HIGHEST

def reference(dual_ops, local_load, rigid_modes, coarse_load, gluing_peer, gluing_sign):
    sign_field = jnp.repeat(gluing_sign.astype(jnp.float32), BLOCK, axis=2)
    peer_table = gluing_peer.reshape(CLUSTERS, SUBS, 4, 4)
    cluster_ids = jnp.arange(CLUSTERS)[:, None] * jnp.ones((1, SUBS), jnp.int32)
    sub_ids = jnp.ones((CLUSTERS, 1), jnp.int32) * jnp.arange(SUBS)[None, :]
    has_peer = jnp.stack([sub_ids > 0, sub_ids < SUBS - 1, cluster_ids > 0, cluster_ids < CLUSTERS - 1], axis=-1)
    block_weight = jnp.where(has_peer, 0.5, 1.0).astype(jnp.float32)
    weights = jnp.broadcast_to(block_weight[:, :, None, :, None], (CLUSTERS, SUBS, 4, 4, BLOCK)).reshape(CLUSTERS, SUBS, M)

    def assemble(local_part):
        breadth = local_part.shape[-1]
        shaped = local_part.reshape(CLUSTERS, SUBS, 4, 4, BLOCK, breadth)
        zero_sub = jnp.zeros((CLUSTERS, 1, 4, BLOCK, breadth), jnp.float32)
        zero_cluster = jnp.zeros((1, SUBS, 4, BLOCK, breadth), jnp.float32)
        incoming = [jnp.concatenate([zero_sub, shaped[:, :-1, :, 1]], axis=1), jnp.concatenate([shaped[:, 1:, :, 0], zero_sub], axis=1), jnp.concatenate([zero_cluster, shaped[:-1, :, :, 3]], axis=0), jnp.concatenate([shaped[1:, :, :, 2], zero_cluster], axis=0)]
        picked = [jnp.take_along_axis(arrived, peer_table[:, :, :, facing][:, :, :, None, None], axis=2) for facing, arrived in enumerate(incoming)]
        return local_part + jnp.stack(picked, axis=3).reshape(CLUSTERS, SUBS, M, breadth)

    def spread(amplitude_blocks):
        local_part = sign_field[..., None] * jnp.einsum('cskm,ckr->csmr', rigid_modes, amplitude_blocks, precision=HIGHEST)
        return assemble(local_part)

    def restrict(field):
        terms = jnp.einsum('cskm,csmr->ckr', rigid_modes, sign_field[..., None] * field, precision=HIGHEST)
        return terms.reshape(CLUSTERS * MODES, -1)
    unit_columns = jnp.eye(CLUSTERS * MODES, dtype=jnp.float32).reshape(CLUSTERS, MODES, CLUSTERS * MODES)
    coarse = restrict(spread(unit_columns))
    factor = jnp.linalg.cholesky(coarse)

    def solve(right_side):
        return jax.scipy.linalg.cho_solve((factor, True), right_side)

    def inner(first_field, second_field):
        return jnp.sum(weights[..., None] * first_field * second_field, axis=(0, 1, 2))
    flat_ops = dual_ops.reshape(CLUSTERS * SUBS, M, M)

    def apply_dual(direction):
        signed = (sign_field[..., None] * direction).astype(jnp.bfloat16)
        flat_signed = signed.reshape(CLUSTERS * SUBS, M, LOADS)
        images = lax.map(lambda operands: jnp.dot(operands[0].astype(jnp.float32), operands[1].astype(jnp.float32), preferred_element_type=jnp.float32), (flat_ops, flat_signed)).reshape(CLUSTERS, SUBS, M, LOADS)
        curvature = jnp.sum(signed.astype(jnp.float32) * images, axis=(0, 1, 2))
        return (curvature, assemble(sign_field[..., None] * images))

    def project(residual):
        amplitudes = solve(restrict(residual))
        projected = residual - spread(amplitudes.reshape(CLUSTERS, MODES, -1))
        return (projected, inner(projected, projected), amplitudes)
    dual_load = assemble(sign_field[..., None] * local_load)
    start_amplitudes = solve(coarse_load.reshape(CLUSTERS * MODES, LOADS))
    multipliers = spread(start_amplitudes.reshape(CLUSTERS, MODES, LOADS))
    residual = dual_load - apply_dual(multipliers)[1]
    projected, norm_now, amplitudes = project(residual)
    direction = projected
    for step_index in range(ITERS):
        curvature, image = apply_dual(direction)
        length = norm_now / curvature
        multipliers = multipliers + length * direction
        residual = residual - length * image
        projected, norm_next, amplitudes = project(residual)
        direction = projected + norm_next / norm_now * direction
        norm_now = norm_next
    return (multipliers, amplitudes.reshape(CLUSTERS, MODES, LOADS))
```

```python
import functools

import jax
import jax.numpy as jnp
from jax import lax
from jax.experimental import pallas as pl
from jax.experimental.pallas import tpu as pltpu
from jax.sharding import PartitionSpec as P

MESH = pl.DeviceIdType.MESH
HIGHEST = lax.Precision.HIGHEST
F32 = jnp.float32
BF16 = jnp.bfloat16
MODES = 6
PAD = 8


def split(value):
    high = value.astype(BF16)
    low = (value - high.astype(F32)).astype(BF16)
    return high, low


def elimination_levels(count):
    levels, step = [], 1
    while step < count:
        levels.append(list(range(step, count, 2 * step)))
        step *= 2
    return levels + [[0]]


def coarse_inverse(tiles):
    count = len(tiles)
    rows = lax.broadcasted_iota(jnp.int32, (PAD, 128), 0)
    lanes = lax.broadcasted_iota(jnp.int32, (PAD, 128), 1)
    left = list(tiles)
    right = [
        jnp.where((lanes == rows + PAD * t) & (rows < MODES), 1.0, 0.0).astype(F32)
        for t in range(count)
    ]
    pattern = [[abs(t - u) <= 1 for u in range(count)] for t in range(count)]
    scale = [jnp.ones((PAD, 128), F32) for _ in range(count)]
    for level in elimination_levels(count):
        touched = {p: [t for t in range(count) if pattern[t][p]] for p in level}
        for mode in range(MODES):
            updates = []
            for p in level:
                column = PAD * p + mode
                factors = {
                    t: jnp.broadcast_to(left[t][:, column : column + 1], (PAD, 128))
                    for t in touched[p]
                }
                inverse = 1.0 / factors[p][mode : mode + 1, :]
                row_left = left[p][mode : mode + 1, :] * inverse
                row_right = right[p][mode : mode + 1, :] * inverse
                factors[p] = jnp.where(rows == mode, 0.0, factors[p])
                scale[p] = jnp.where(rows == mode, inverse, scale[p])
                updates.append((factors, row_left, row_right))
            for factors, row_left, row_right in updates:
                for t, factor in factors.items():
                    left[t] = left[t] - factor * row_left
                    right[t] = right[t] - factor * row_right
        for p in level:
            for t in touched[p]:
                for u in range(count):
                    pattern[t][u] = pattern[t][u] or pattern[p][u]
    return [r * k for r, k in zip(right, scale)]


def kernel(
    C,
    S,
    peer,
    sign,
    dual_hbm,
    load_hbm,
    modes_hbm,
    cload_hbm,
    out_hbm,
    amp_out,
    dual,
    load,
    modes,
    cload,
    lam,
    res,
    z0,
    z1,
    im0,
    im1,
    im2,
    halo00,
    halo01,
    halo02,
    halo03,
    halo10,
    halo11,
    halo12,
    halo13,
    rhs,
    gt,
    t3,
    cinv,
    ka,
    kb,
    ra,
    rb,
    lsem,
    osem,
    hsend,
    hrecv,
    asend,
    arecv,
    bsend,
    brecv,
):
    c = lax.axis_index("cluster")
    s = lax.axis_index("sub")
    has = [s > 0, s < S - 1, c > 0, c < C - 1]
    halo = [[halo00, halo01, halo02, halo03], [halo10, halo11, halo12, halo13]]

    cp_modes = pltpu.make_async_copy(modes_hbm, modes, lsem.at[0])
    cp_cload = pltpu.make_async_copy(cload_hbm, cload, lsem.at[1])
    cp_dual = pltpu.make_async_copy(dual_hbm, dual, lsem.at[2])
    cp_load = pltpu.make_async_copy(load_hbm, load, lsem.at[3])
    cp_modes.start()
    cp_cload.start()
    cp_dual.start()
    cp_load.start()

    barrier = pltpu.get_barrier_semaphore()

    def greet_sub(i, carry):
        pl.semaphore_signal(
            barrier, inc=1, device_id=(c, lax.rem(s + i, S)), device_id_type=MESH
        )
        return carry

    def greet_cluster(i, carry):
        pl.semaphore_signal(
            barrier, inc=1, device_id=(lax.rem(c + i, C), s), device_id_type=MESH
        )
        return carry

    lax.fori_loop(1, S, greet_sub, 0)
    lax.fori_loop(1, C, greet_cluster, 0)

    def send_sub(buf, k):
        def body(i, carry):
            pltpu.make_async_remote_copy(
                src_ref=buf.at[s],
                dst_ref=buf.at[s],
                send_sem=asend.at[k],
                recv_sem=arecv.at[k],
                device_id=(c, lax.rem(s + i, S)),
                device_id_type=MESH,
            ).start()
            return carry

        lax.fori_loop(1, S, body, 0)

    def send_cluster(buf, k):
        def body(i, carry):
            pltpu.make_async_remote_copy(
                src_ref=buf.at[c],
                dst_ref=buf.at[c],
                send_sem=bsend.at[k],
                recv_sem=brecv.at[k],
                device_id=(lax.rem(c + i, C), s),
                device_id_type=MESH,
            ).start()
            return carry

        lax.fori_loop(1, C, body, 0)

    def wait_bytes(buf, count, sem):
        part = buf.at[pl.ds(0, count - 1)]
        pltpu.make_async_copy(part, part, sem).wait()

    def sum_sub(buf):
        total = buf[0]
        for i in range(1, S):
            total = total + buf[i]
        return total

    def halo_copy(src, x, f):
        device = [(c, s - 1), (c, s + 1), (c - 1, s), (c + 1, s)][f]
        return pltpu.make_async_remote_copy(
            src_ref=src.at[f],
            dst_ref=halo[x][f ^ 1],
            send_sem=hsend.at[x, f],
            recv_sem=hrecv.at[x, f ^ 1],
            device_id=device,
            device_id_type=MESH,
        )

    def halo_arrived(src, x, f):
        pltpu.make_async_copy(halo[x][f], halo[x][f], hrecv.at[x, f]).wait()

    for f in range(4):

        @pl.when(jnp.logical_not(has[f]))
        def _():
            for x in range(2):
                halo[x][f][...] = jnp.zeros((4, 128, 128), F32)

    cp_modes.wait()
    cp_cload.wait()
    size = modes.shape[1]
    rows = jnp.concatenate([modes[...], jnp.zeros((PAD - MODES, size), F32)], axis=0)
    face = (lax.broadcasted_iota(jnp.int32, (PAD, size), 1) // 128) % 4
    at_rim0 = jnp.where(s > 0, 0.0, 1.0)
    at_rim1 = jnp.where(s < S - 1, 0.0, 1.0)
    low_on = jnp.where(c > 0, 1.0, 0.0)
    high_on = jnp.where(c < C - 1, 1.0, 0.0)
    rows2 = jnp.where(face == 2, rows, 0.0)
    rows3 = jnp.where(face == 3, rows, 0.0)
    own = jnp.where(face >= 2, rows, jnp.where(face == 0, rows * at_rim0, rows * at_rim1))
    span = jnp.concatenate([-low_on * rows2, own, -high_on * rows3], axis=0)

    coarse_row = lax.dot_general(
        rows, span, (((1,), (1,)), ((), ())), precision=HIGHEST, preferred_element_type=F32
    )
    coarse_row = jnp.concatenate([coarse_row, jnp.zeros((PAD, 128 - 3 * PAD), F32)], axis=1)
    shift = lax.rem(PAD * c + 128 - PAD, 128)
    ka[s] = pltpu.roll(coarse_row, shift, 1)

    pl.semaphore_wait(barrier, S - 1 + C - 1)
    send_sub(ka, 0)

    by_face = [
        jnp.concatenate(
            [part[:, 128 * (4 * k + f) : 128 * (4 * k + f + 1)] for f in range(4) for k in range(4)],
            axis=1,
        )
        for part in (own, rows2, rows3)
    ]
    t3_high, t3_low = split(jnp.concatenate(by_face, axis=0))
    t3[...] = jnp.concatenate([t3_high, t3_low], axis=0)
    span_high = span.astype(BF16).astype(F32)
    wide = jnp.concatenate(
        [span_high, span - span_high, span_high, jnp.zeros((128 - 9 * PAD, size), F32)], axis=0
    )
    for b in range(16):
        gt[b // 4, b % 4] = wide[:, 128 * b : 128 * (b + 1)].T.astype(BF16)

    wait_bytes(ka, S, arecv.at[0])
    kb[c, 0:PAD] = sum_sub(ka)
    kb[c, PAD : 2 * PAD] = jnp.concatenate(
        [cload[...], jnp.zeros((PAD - MODES, 128), F32)], axis=0
    )
    send_cluster(kb, 0)
    wait_bytes(kb, C, brecv.at[0])

    inverse = coarse_inverse([kb[t, 0:PAD] for t in range(C)])
    zero_tile = jnp.zeros((PAD, 128), F32)
    cinv[0:PAD] = zero_tile
    for t in range(C):
        cinv[PAD * (t + 1) : PAD * (t + 2)] = inverse[t]
    cinv[PAD * (C + 1) : PAD * (C + 2)] = zero_tile

    def stacked(parts):
        value = jnp.concatenate(parts, axis=0)
        if value.shape[0] < 128:
            value = jnp.concatenate([value, jnp.zeros((128 - value.shape[0], 128), F32)], axis=0)
        return value

    def near_solve(right):
        return jnp.dot(cinv[pl.ds(PAD * c, 3 * PAD), :], right, precision=HIGHEST)

    def packed(amplitudes):
        high = amplitudes.astype(BF16).astype(F32)
        return jnp.concatenate(
            [high, high, amplitudes - high, jnp.zeros((128 - 9 * PAD, 128), F32)], axis=0
        ).astype(BF16)

    def spread(weights, k, f):
        return jnp.dot(gt[k, f], weights, preferred_element_type=F32)

    def restricted(field):
        value = field[...].reshape(size, 128)
        high, low = split(value)
        pair = jnp.dot(
            t3[...], jnp.concatenate([high, low], axis=1), preferred_element_type=F32
        )
        half = 3 * PAD
        return pair[:half, :128] + (pair[half:, :128] + pair[:half, 128:]) + pair[half:, 128:]

    def joined(buf):
        parts = []
        for t in range(C):
            part = buf[t, 0:PAD]
            if t > 0:
                part = part - buf[t - 1, 2 * PAD : 3 * PAD]
            if t < C - 1:
                part = part - buf[t + 1, PAD : 2 * PAD]
            parts.append(part)
        return stacked(parts)

    def scalar_total(buf, row):
        total = buf[0, row : row + 1]
        for t in range(1, C):
            total = total + buf[t, row : row + 1]
        return total

    row_ids = lax.broadcasted_iota(jnp.int32, (3 * PAD, 128), 0)

    def reduce_start(k, terms, scalars):
        for row, value in scalars:
            terms = jnp.where(row_ids == row, value, terms)
        ra[k, s] = terms
        send_sub(ra.at[k], k + 1)

    def reduce_end(k):
        wait_bytes(ra.at[k], S, arecv.at[k + 1])
        rb[k, c] = sum_sub(ra.at[k])
        send_cluster(rb.at[k], k + 1)
        wait_bytes(rb.at[k], C, brecv.at[k + 1])

    half_on = [jnp.where(has[f], 0.5, 1.0) for f in range(4)]

    def column_sum(parts):
        return jnp.sum(parts, axis=0, keepdims=True)

    start = near_solve(stacked([kb[t, PAD : 2 * PAD] for t in range(C)]))
    weights = packed(start)
    for b in range(16):
        k, f = b // 4, b % 4
        value = spread(weights, k, f)
        lam[k, f] = value
        rhs[k, f, :, 0:128] = value.astype(BF16)

    cp_dual.wait()
    cp_load.wait()
    for f in range(4):
        part = jnp.dot(
            dual[:, f].reshape(size // 4, size),
            rhs[:, :, :, 0:128].reshape(size, 128),
            preferred_element_type=F32,
        )
        im0[f] = load[:, f] - part.reshape(4, 128, 128)

        @pl.when(has[f])
        def _():
            halo_copy(im0, 0, f).start()

    reduce_start(0, restricted(im0), [])
    reduce_end(0)
    coarse_now = joined(rb.at[0])
    weights = packed(near_solve(coarse_now))
    for f in range(4):

        @pl.when(has[f])
        def _():
            halo_arrived(im0, 0, f)

    norm = jnp.zeros((PAD, 128), F32)
    for b in range(16):
        k, f = b // 4, b % 4
        value = im0[f, k] - halo[0][f][peer[0, 0, b]]
        res[k, f] = value
        value = value - spread(weights, k, f)
        z0[k, f] = value
        rhs[k, f, :, 0:128] = value.astype(BF16)
        norm = norm + half_on[f] * jnp.sum((value * value).reshape(16, PAD, 128), axis=0)
    norm = column_sum(norm)

    curvature = jnp.zeros((PAD, 128), F32)
    for f in range(4):
        part = jnp.dot(
            dual[:, f].reshape(size // 4, size),
            rhs[:, :, :, 0:128].reshape(size, 128),
            preferred_element_type=F32,
        ).reshape(4, 128, 128)
        im1[f] = part
        signed = rhs[:, f, :, 0:128].astype(F32)
        curvature = curvature + jnp.sum((signed * part).reshape(64, PAD, 128), axis=0)

        @pl.when(has[f])
        def _():
            halo_copy(im1, 1, f).start()

    reduce_start(1, restricted(im1), [(6, norm), (7, column_sum(curvature))])
    reduce_end(1)
    norm_now = scalar_total(rb.at[1], 6)
    curvature_now = scalar_total(rb.at[1], 7)
    length = norm_now / curvature_now
    coarse_image = joined(rb.at[1])
    coarse_now = coarse_now - length * coarse_image
    weights = packed(near_solve(coarse_now))
    for f in range(4):

        @pl.when(has[f])
        def _():
            halo_arrived(im1, 1, f)

    norm = jnp.zeros((PAD, 128), F32)
    cross = jnp.zeros((PAD, 128), F32)
    for b in range(16):
        k, f = b // 4, b % 4
        value = res[k, f] - length * (im1[f, k] - halo[1][f][peer[0, 0, b]])
        value = value - spread(weights, k, f)
        z1[k, f] = value
        high, low = split(value)
        rhs[k, f, :, 0:128] = high
        rhs[k, f, :, 128:256] = low
        lam[k, f] = lam[k, f] + length * z0[k, f]
        norm = norm + half_on[f] * jnp.sum((value * value).reshape(16, PAD, 128), axis=0)
        cross = cross + jnp.sum((value * im1[f, k]).reshape(16, PAD, 128), axis=0)

    curvature = jnp.zeros((PAD, 128), F32)
    for f in range(4):
        pair = jnp.dot(
            dual[:, f].reshape(size // 4, size),
            rhs[...].reshape(size, 256),
            preferred_element_type=F32,
        )
        part = (pair[:, :128] + pair[:, 128:]).reshape(4, 128, 128)
        im2[f] = part
        curvature = curvature + jnp.sum((z1[:, f] * part).reshape(64, PAD, 128), axis=0)

    reduce_start(
        2,
        restricted(im2),
        [(6, column_sum(norm)), (7, column_sum(curvature)), (14, column_sum(cross))],
    )
    reduce_end(2)
    norm_next = scalar_total(rb.at[2], 6)
    ratio = norm_next / norm_now
    curvature_next = (
        scalar_total(rb.at[2], 7)
        + 2.0 * ratio * scalar_total(rb.at[2], 14)
        + ratio * ratio * curvature_now
    )
    length = norm_next / curvature_next
    coarse_now = coarse_now - length * (joined(rb.at[2]) + ratio * coarse_image)
    last = jnp.dot(cinv[pl.ds(PAD * (c + 1), PAD), :], coarse_now, precision=HIGHEST)
    amp_out[0] = last[:MODES]

    copies = []
    for b in range(16):
        k, f = b // 4, b % 4
        turned = sign[0, 0, b].astype(F32)
        value = lam[k, f] + length * (z1[k, f] + ratio * z0[k, f])
        lam[k, f] = turned * value
        copy = pltpu.make_async_copy(lam.at[k, f], out_hbm.at[k, f], osem.at[b])
        copy.start()
        copies.append(copy)

    for k in range(4):
        wait_bytes(ka if k == 0 else ra.at[k - 1], S, asend.at[k])
        wait_bytes(kb if k == 0 else rb.at[k - 1], C, bsend.at[k])
    for f in range(4):

        @pl.when(has[f])
        def _():
            halo_copy(im0, 0, f).wait_send()
            halo_copy(im1, 1, f).wait_send()

    for copy in copies:
        copy.wait()


def per_device(C, S, dual_ops, local_load, rigid_modes, coarse_load, gluing_peer, gluing_sign):
    size = dual_ops.shape[-1]
    block = size // 16
    loads = local_load.shape[-1]
    any_space = pl.BlockSpec(memory_space=pl.ANY)
    smem = pl.BlockSpec(memory_space=pltpu.SMEM)
    field = pltpu.VMEM((4, 4, block, loads), F32)
    multipliers, amplitudes = pl.pallas_call(
        functools.partial(kernel, C, S),
        out_shape=(
            jax.ShapeDtypeStruct((4, 4, block, loads), F32),
            jax.ShapeDtypeStruct((1, MODES, loads), F32),
        ),
        in_specs=[smem, smem] + [any_space] * 4,
        out_specs=(any_space, pl.BlockSpec(memory_space=pltpu.VMEM)),
        scratch_shapes=[
            pltpu.VMEM((4, 4, block, size), BF16),
            field,
            pltpu.VMEM((MODES, size), F32),
            pltpu.VMEM((MODES, loads), F32),
            field,
            field,
            field,
            field,
            field,
            field,
            field,
        ]
        + [pltpu.VMEM((4, block, loads), F32)] * 8
        + [
            pltpu.VMEM((4, 4, block, 2 * loads), BF16),
            pltpu.VMEM((4, 4, block, 128), BF16),
            pltpu.VMEM((6 * PAD, size), BF16),
            pltpu.VMEM((PAD * (C + 2), 128), F32),
            pltpu.VMEM((S, PAD, 128), F32),
            pltpu.VMEM((C, 2 * PAD, 128), F32),
            pltpu.VMEM((3, S, 3 * PAD, 128), F32),
            pltpu.VMEM((3, C, 3 * PAD, 128), F32),
            pltpu.SemaphoreType.DMA((4,)),
            pltpu.SemaphoreType.DMA((16,)),
            pltpu.SemaphoreType.DMA((2, 4)),
            pltpu.SemaphoreType.DMA((2, 4)),
            pltpu.SemaphoreType.DMA((4,)),
            pltpu.SemaphoreType.DMA((4,)),
            pltpu.SemaphoreType.DMA((4,)),
            pltpu.SemaphoreType.DMA((4,)),
        ],
        compiler_params=pltpu.CompilerParams(
            collective_id=0, has_side_effects=True, vmem_limit_bytes=48 * 1024 * 1024
        ),
    )(
        gluing_peer,
        gluing_sign,
        dual_ops.reshape(4, 4, block, size),
        local_load.reshape(4, 4, block, loads),
        rigid_modes[0, 0],
        coarse_load[0],
    )
    return multipliers.reshape(1, 1, size, loads), amplitudes


def solution(mesh):
    return jax.shard_map(
        functools.partial(per_device, mesh.shape["cluster"], mesh.shape["sub"]),
        mesh=mesh,
        in_specs=(
            P("cluster", "sub", None, None),
            P("cluster", "sub", None, None),
            P("cluster", "sub", None, None),
            P("cluster", None, None),
            P("cluster", "sub", None),
            P("cluster", "sub", None),
        ),
        out_specs=(P("cluster", "sub", None, None), P("cluster", None, None)),
        check_vma=False,
    )
```

```python
import functools
import types

import jax
import jax.numpy as jnp
from jax import lax
from jax.experimental import pallas as pl
from jax.experimental.pallas import tpu as pltpu
from jax.sharding import PartitionSpec as P

MESH = pl.DeviceIdType.MESH
HIGHEST = lax.Precision.HIGHEST
F32 = jnp.float32
BF16 = jnp.bfloat16
MODES = 6
PAD = 8


def split(value):
    high = value.astype(BF16)
    low = (value - high.astype(F32)).astype(BF16)
    return high, low


def elimination_levels(count):
    levels, step = [], 1
    while step < count:
        levels.append(list(range(step, count, 2 * step)))
        step *= 2
    return levels + [[0]]


def coarse_inverse(tiles):
    count = len(tiles)
    rows = lax.broadcasted_iota(jnp.int32, (PAD, 128), 0)
    lanes = lax.broadcasted_iota(jnp.int32, (PAD, 128), 1)
    left = list(tiles)
    right = [
        jnp.where((lanes == rows + PAD * t) & (rows < MODES), 1.0, 0.0).astype(F32)
        for t in range(count)
    ]
    pattern = [[abs(t - u) <= 1 for u in range(count)] for t in range(count)]
    scale = [jnp.ones((PAD, 128), F32) for _ in range(count)]
    for level in elimination_levels(count):
        touched = {p: [t for t in range(count) if pattern[t][p]] for p in level}
        for mode in range(MODES):
            updates = []
            for p in level:
                column = PAD * p + mode
                factors = {
                    t: jnp.broadcast_to(left[t][:, column : column + 1], (PAD, 128))
                    for t in touched[p]
                }
                inverse = 1.0 / factors[p][mode : mode + 1, :]
                row_left = left[p][mode : mode + 1, :] * inverse
                row_right = right[p][mode : mode + 1, :] * inverse
                factors[p] = jnp.where(rows == mode, 0.0, factors[p])
                scale[p] = jnp.where(rows == mode, inverse, scale[p])
                updates.append((factors, row_left, row_right))
            for factors, row_left, row_right in updates:
                for t, factor in factors.items():
                    left[t] = left[t] - factor * row_left
                    right[t] = right[t] - factor * row_right
        for p in level:
            for t in touched[p]:
                for u in range(count):
                    pattern[t][u] = pattern[t][u] or pattern[p][u]
    return [r * k for r, k in zip(right, scale)]


NAMES = (
    "peer_hbm",
    "dual_hbm",
    "load_hbm",
    "modes_hbm",
    "cload_hbm",
    "lam_hbm",
    "z0_hbm",
    "w_hbm",
    "last_out",
    "peer",
    "dual",
    "load",
    "modes",
    "cload",
    "lam",
    "z0",
    "y",
    "im0",
    "h00",
    "h01",
    "h02",
    "h03",
    "h10",
    "h11",
    "h12",
    "h13",
    "a0",
    "a1",
    "a2",
    "a3",
    "r0",
    "r1",
    "r2",
    "r3",
    "rhs",
    "basis",
    "t3",
    "d3",
    "cinv",
    "coef",
    "msg",
    "ka",
    "kb",
    "eb",
    "ra0",
    "rb0",
    "ra2",
    "rb2",
    "ra3",
    "ub3",
    "rb3",
    "sa",
    "sb",
    "lsem",
    "osem",
    "hsend",
    "hrecv",
    "gsend",
    "grecv",
    "asend",
    "arecv",
    "bsend",
    "brecv",
    "ksend",
    "krecv",
    "esend",
    "erecv",
)


def kernel(C, S, *refs):
    r = types.SimpleNamespace(**dict(zip(NAMES, refs)))
    c = lax.axis_index("cluster")
    s = lax.axis_index("sub")
    Z = C // 2
    z, core = c // 2, lax.rem(c, 2)
    has = [s > 0, s < S - 1, c > 0, c < C - 1]
    towards = [(c, s - 1), (c, s + 1), (c - 1, s), (c + 1, s)]
    halo = [[r.h00, r.h01, r.h02, r.h03], [r.h10, r.h11, r.h12, r.h13]]
    near_modes = [r.a0, r.a1, r.a2, r.a3]
    turned_modes = [r.r0, r.r1, r.r2, r.r3]
    size = r.dual.shape[3]

    cp_modes = pltpu.make_async_copy(r.modes_hbm, r.modes, r.lsem.at[0])
    cp_cload = pltpu.make_async_copy(r.cload_hbm, r.cload, r.lsem.at[1])
    cp_dual = pltpu.make_async_copy(r.dual_hbm, r.dual, r.lsem.at[2])
    cp_load = [
        pltpu.make_async_copy(r.load_hbm.at[:, f], r.load.at[f], r.lsem.at[3 + f]) for f in range(4)
    ]
    cp_peer = pltpu.make_async_copy(r.peer_hbm, r.peer, r.lsem.at[7])
    cp_modes.start()
    cp_peer.start()
    cp_cload.start()
    for copy in cp_load:
        copy.start()
    cp_dual.start()

    barrier = pltpu.get_barrier_semaphore()

    def greet_sub(i, carry):
        pl.semaphore_signal(
            barrier, inc=1, device_id=(c, lax.rem(s + i, S)), device_id_type=MESH
        )
        return carry

    def greet_cluster(i, carry):
        pl.semaphore_signal(
            barrier, inc=1, device_id=(lax.rem(c + i, C), s), device_id_type=MESH
        )
        return carry

    lax.fori_loop(1, S, greet_sub, 0)
    lax.fori_loop(1, C, greet_cluster, 0)

    def send(src, dst, send_sem, recv_sem, device):
        pltpu.make_async_remote_copy(
            src_ref=src,
            dst_ref=dst,
            send_sem=send_sem,
            recv_sem=recv_sem,
            device_id=device,
            device_id_type=MESH,
        ).start()

    def wait_bytes(part, sem):
        pltpu.make_async_copy(part, part, sem).wait()

    def sub_start(buf, k):
        def body(i, carry):
            send(buf.at[s], buf.at[s], r.asend.at[k], r.arecv.at[k], (c, lax.rem(s + i, S)))
            return carry

        lax.fori_loop(1, S, body, 0)

    def sub_total(buf, k):
        wait_bytes(buf.at[pl.ds(0, S - 1)], r.arecv.at[k])
        total = buf[0]
        for i in range(1, S):
            total = total + buf[i]
        return total

    def chips_start(buf, k):
        def body(i, carry):
            there = lax.rem(z + i, Z) * 2 + core
            send(buf.at[core, z], buf.at[core, z], r.bsend.at[k], r.brecv.at[k], (there, s))
            return carry

        lax.fori_loop(1, Z, body, 0)

    def cores_start(buf, k):
        wait_bytes(buf.at[0, pl.ds(0, Z - 1)], r.brecv.at[k])
        send(buf.at[core], buf.at[core], r.ksend.at[k], r.krecv.at[k], (2 * z + 1 - core, s))

    def cores_end(buf, k):
        wait_bytes(buf.at[0], r.krecv.at[k])

    def cluster_start(src, buf, k):
        def body(i, carry):
            there = lax.rem(c + i, C)
            send(src(there), buf.at[c], r.bsend.at[k], r.brecv.at[k], (there, s))
            return carry

        lax.fori_loop(1, C, body, 0)

    def cluster_total(buf, k):
        wait_bytes(buf.at[pl.ds(0, C - 1)], r.brecv.at[k])
        total = buf[0]
        for t in range(1, C):
            total = total + buf[t]
        return total

    def at_cluster(buf, t):
        return buf.at[t % 2, t // 2]

    def halo_copy(src, x, f):
        return pltpu.make_async_remote_copy(
            src_ref=src.at[f],
            dst_ref=halo[x][f ^ 1],
            send_sem=r.hsend.at[x, f],
            recv_sem=r.hrecv.at[x, f ^ 1],
            device_id=towards[f],
            device_id_type=MESH,
        )

    def modes_copy(f):
        return pltpu.make_async_remote_copy(
            src_ref=r.msg.at[f],
            dst_ref=near_modes[f ^ 1],
            send_sem=r.gsend.at[f],
            recv_sem=r.grecv.at[f ^ 1],
            device_id=towards[f],
            device_id_type=MESH,
        )

    for f in range(4):

        @pl.when(jnp.logical_not(has[f]))
        def _():
            for x in range(2):
                halo[x][f][...] = jnp.zeros((4, 128, 128), F32)
            near_modes[f][...] = jnp.zeros((128, 128), F32)

    r.coef[...] = jnp.zeros(r.coef.shape, F32)

    cp_modes.wait()
    cp_peer.wait()
    rows = jnp.concatenate([r.modes[:, b] for b in range(16)], axis=1)
    rows = jnp.concatenate([rows, jnp.zeros((PAD - MODES, size), F32)], axis=0)
    face = (lax.broadcasted_iota(jnp.int32, (PAD, size), 1) // 128) % 4
    at_rim0 = jnp.where(s > 0, 0.0, 1.0)
    at_rim1 = jnp.where(s < S - 1, 0.0, 1.0)
    low_on = jnp.where(c > 0, 1.0, 0.0)
    high_on = jnp.where(c < C - 1, 1.0, 0.0)
    rows2 = jnp.where(face == 2, rows, 0.0)
    rows3 = jnp.where(face == 3, rows, 0.0)
    own = jnp.where(face >= 2, rows, jnp.where(face == 0, rows * at_rim0, rows * at_rim1))
    span = jnp.concatenate([-low_on * rows2, own, -high_on * rows3], axis=0)

    coarse_row = lax.dot_general(
        rows, span, (((1,), (1,)), ((), ())), precision=HIGHEST, preferred_element_type=F32
    )
    coarse_row = jnp.concatenate([coarse_row, jnp.zeros((PAD, 128 - 3 * PAD), F32)], axis=1)
    r.ka[s] = pltpu.roll(coarse_row, lax.rem(PAD * c + 128 - PAD, 128), 1)

    cp_cload.wait()
    r.eb[c] = jnp.concatenate(
        [r.cload[:, 0], jnp.zeros((PAD - MODES, 128), F32)], axis=0
    )

    by_face = [
        jnp.concatenate(
            [part[:, 128 * (4 * k + f) : 128 * (4 * k + f + 1)] for f in range(4) for k in range(4)],
            axis=1,
        )
        for part in (own, rows2, rows3)
    ]
    t3_high, t3_low = split(jnp.concatenate(by_face, axis=0))
    r.t3[...] = jnp.concatenate([t3_high, t3_low], axis=0)
    span_high = span.astype(BF16).astype(F32)
    gap = jnp.zeros((PAD, size), F32)
    wide = jnp.concatenate(
        [span_high, gap, span - span_high, gap, span_high, gap, gap, gap, gap, gap], axis=0
    )
    for b in range(16):
        r.basis[b // 4, b % 4, :, 256:384] = wide[:, 128 * b : 128 * (b + 1)].T.astype(BF16)

    lanes = lax.broadcasted_iota(jnp.int32, (128, 128), 1)

    def tripled(value):
        high = value.astype(BF16).astype(F32)
        return (high + pltpu.roll(value - high, 32, 1) + pltpu.roll(high, 64, 1)).astype(BF16)

    cp_dual.wait()
    turned = []
    for f in range(4):
        part = jnp.dot(
            r.dual[:, f].reshape(size // 4, size),
            r.basis[:, :, :, 256:384].reshape(size, 128),
            preferred_element_type=F32,
        ).reshape(4, 128, 128)
        side = None
        for k in range(4):
            block = jnp.where(lanes < 3 * PAD, part[k] + pltpu.roll(part[k], 96, 1), 0.0)
            r.im0[f, k] = block
            turned.append(block.T[0 : 3 * PAD])
            r.basis[k, f, :, 0:128] = tripled(block)
            side = block if side is None else side + pltpu.roll(block, 32 * k, 1)
        r.msg[f] = side
    d3_high, d3_low = split(jnp.concatenate(turned, axis=1))
    r.d3[...] = jnp.concatenate([d3_high, d3_low], axis=0)

    def rows_times(left, high, low):
        pair = jnp.dot(
            left[...], jnp.concatenate([high, low], axis=1), preferred_element_type=F32
        )
        half = 3 * PAD
        return pair[:half, :128] + (pair[half:, :128] + pair[:half, 128:]) + pair[half:, 128:]

    def field_terms(left, field):
        return rows_times(left, *split(field[...].reshape(size, 128)))

    for copy in cp_load:
        copy.wait()
    mode_terms = field_terms(r.t3, r.im0)
    r.ra0[s, 0 : 3 * PAD] = field_terms(r.t3, r.load)
    r.ra0[s, 3 * PAD : 4 * PAD] = (
        mode_terms[0:PAD]
        + pltpu.roll(mode_terms[PAD : 2 * PAD], 32, 1)
        + pltpu.roll(mode_terms[2 * PAD : 3 * PAD], 64, 1)
    )

    pl.semaphore_wait(barrier, S - 1 + C - 1)
    sub_start(r.ka, 0)
    sub_start(r.ra0, 1)

    def send_e(i, carry):
        send(r.eb.at[c], r.eb.at[c], r.esend, r.erecv, (lax.rem(c + i, C), s))
        return carry

    lax.fori_loop(1, C, send_e, 0)

    for f in range(4):

        @pl.when(has[f])
        def _():
            halo_copy(r.load, 0, f).start()

    r.kb[c] = sub_total(r.ka, 0)
    cluster_start(lambda there: r.kb.at[c], r.kb, 0)
    r.rb0[core, z] = sub_total(r.ra0, 1)
    chips_start(r.rb0, 1)
    for f in range(4):

        @pl.when(has[f])
        def _():
            modes_copy(f).start()

    cores_start(r.rb0, 1)
    wait_bytes(r.kb.at[pl.ds(0, C - 1)], r.brecv.at[0])
    inverse = coarse_inverse([r.kb[t] for t in range(C)])
    zero_tile = jnp.zeros((PAD, 128), F32)
    r.cinv[0:PAD] = zero_tile
    for t in range(C):
        r.cinv[PAD * (t + 1) : PAD * (t + 2)] = inverse[t]
    r.cinv[PAD * (C + 1) : PAD * (C + 2)] = zero_tile

    def filled(value):
        if value.shape[0] < 128:
            value = jnp.concatenate([value, jnp.zeros((128 - value.shape[0], 128), F32)], axis=0)
        return value

    def solve(right):
        return jnp.dot(r.cinv[PAD : PAD * (C + 1), :], right, precision=HIGHEST)

    def keep(k, value):
        r.coef[k, 2 * PAD : PAD * (C + 2)] = value

    def near(k, offset):
        return r.coef[k, pl.ds(PAD * (c + 1 + offset), 3 * PAD), :]

    def packed(value):
        high = value.astype(BF16).astype(F32)
        empty = jnp.zeros((PAD, 128), F32)
        return jnp.concatenate(
            [high, empty, high, empty, value - high, empty, empty, empty, empty, empty], axis=0
        ).astype(BF16)

    wait_bytes(r.eb.at[pl.ds(0, C - 1)], r.erecv)
    start = solve(filled(jnp.concatenate([r.eb[t] for t in range(C)], axis=0)))
    keep(0, start)
    start = filled(start)

    for f in range(4):

        @pl.when(has[f])
        def _():
            wait_bytes(halo[0][f], r.hrecv.at[0, f])
            wait_bytes(near_modes[f], r.grecv.at[f])

    start_here = packed(near(0, 0))
    start_near = [start_here, start_here, packed(near(0, -1)), packed(near(0, 1))]
    for f in range(4):
        for j in range(4):
            group = r_f = near_modes[f][...]
            if j:
                group = pltpu.roll(r_f, 128 - 32 * j, 1)
            turned_modes[f][j] = jnp.where(lanes < 3 * PAD, group, 0.0)
        for k in range(4):
            r.basis[k, f, :, 128:256] = tripled(turned_modes[f][r.peer[0, 0, 4 * k + f]])
        image = jnp.dot(
            r.basis[:, f, :, 0:256].reshape(size // 4, 256),
            jnp.concatenate([start_here, -start_near[f]], axis=0),
            preferred_element_type=F32,
        ).reshape(4, 128, 128)
        spread_start = jnp.dot(
            r.basis[:, f, :, 256:384].reshape(size // 4, 128),
            start_here,
            preferred_element_type=F32,
        ).reshape(4, 128, 128)
        r.lam[f] = spread_start
        for k in range(4):
            r.z0[f, k] = r.load[f, k] - halo[0][f][r.peer[0, 0, 4 * k + f]] - image[k]

    out_lam = pltpu.make_async_copy(r.lam, r.lam_hbm, r.osem.at[0])
    out_lam.start()

    def joined(tile):
        parts = []
        for t in range(C):
            part = tile(t, 0)
            if t > 0:
                part = part - tile(t - 1, 2)
            if t < C - 1:
                part = part - tile(t + 1, 1)
            parts.append(part)
        return filled(jnp.concatenate(parts, axis=0))

    def term(buf):
        return lambda t, kind: at_cluster(buf, t)[PAD * kind : PAD * (kind + 1)]

    tile_lanes = lax.broadcasted_iota(jnp.int32, (PAD, 128), 1)

    def mode_term(t, kind):
        value = at_cluster(r.rb0, t)[3 * PAD : 4 * PAD]
        value = jnp.where((tile_lanes >= 32 * kind) & (tile_lanes < 32 * kind + 3 * PAD), value, 0.0)
        turn = (PAD * (t - 1) - 32 * kind) % 128
        return pltpu.roll(value, turn, 1) if turn else value

    cores_end(r.rb0, 1)
    gfg = joined(mode_term)
    coarse_now = joined(term(r.rb0)) - jnp.dot(gfg, start, precision=HIGHEST)
    first = solve(coarse_now)
    keep(1, first)
    weights = packed(near(1, 0))

    half_on = [jnp.where(has[f], 0.5, 1.0) for f in range(4)]

    def folded(value):
        return jnp.sum(value.reshape(-1, PAD, 128), axis=0)

    def column_sum(parts):
        return jnp.sum(parts, axis=0, keepdims=True)

    def spread(weights, f):
        return jnp.dot(
            r.basis[:, f, :, 256:384].reshape(size // 4, 128), weights, preferred_element_type=F32
        ).reshape(4, 128, 128)

    row_ids = lax.broadcasted_iota(jnp.int32, (3 * PAD, 128), 0)

    def with_rows(terms, scalars):
        for row, value in scalars:
            terms = jnp.where(row_ids == row, value, terms)
        return terms

    norm = jnp.zeros((PAD, 128), F32)
    for f in range(4):
        value = r.z0[f] - spread(weights, f)
        r.z0[f] = value
        r.rhs[:, f, :, 0:128] = value.astype(BF16)
        norm = norm + half_on[f] * folded(value * value)
    out_z0 = pltpu.make_async_copy(r.z0, r.z0_hbm, r.osem.at[1])
    out_z0.start()
    r.ra2[s] = with_rows(field_terms(r.d3, r.z0), [(6, column_sum(norm))])
    sub_start(r.ra2, 2)

    for f in range(4):
        r.im0[f] = jnp.dot(
            r.dual[:, f].reshape(size // 4, size),
            r.rhs[:, :, :, 0:128].reshape(size, 128),
            preferred_element_type=F32,
        ).reshape(4, 128, 128)

        @pl.when(has[f])
        def _():
            halo_copy(r.im0, 1, f).start()

    r.rb2[core, z] = sub_total(r.ra2, 2)
    chips_start(r.rb2, 2)

    for f in range(4):

        @pl.when(has[f])
        def _():
            wait_bytes(halo[1][f], r.hrecv.at[1, f])

    square = jnp.zeros((PAD, 128), F32)
    cross = jnp.zeros((PAD, 128), F32)
    for f in range(4):
        for k in range(4):
            value = r.im0[f, k] - halo[1][f][r.peer[0, 0, 4 * k + f]]
            r.y[f, k] = value
            high, low = split(value)
            r.rhs[k, f, :, 0:128] = high
            r.rhs[k, f, :, 128:256] = low
            square = square + half_on[f] * folded(value * value)
            cross = cross + half_on[f] * folded(value * r.z0[f, k])
    r.ra3[s] = with_rows(
        field_terms(r.d3, r.y), [(6, column_sum(square)), (7, column_sum(cross))]
    )
    sub_start(r.ra3, 3)

    energy = jnp.zeros((PAD, 128), F32)
    for f in range(4):
        pair = jnp.dot(
            r.dual[:, f].reshape(size // 4, size),
            r.rhs[...].reshape(size, 256),
            preferred_element_type=F32,
        )
        part = (pair[:, :128] + pair[:, 128:]).reshape(4, 128, 128)
        energy = energy + folded(r.y[f] * part)
    r.sa[s] = column_sum(energy)
    sub_start(r.sa, 4)

    cores_start(r.rb2, 2)
    cores_end(r.rb2, 2)
    norm_now = at_cluster(r.rb2, 0)[6:7]
    for t in range(1, C):
        norm_now = norm_now + at_cluster(r.rb2, t)[6:7]
    parts = []
    for t in range(C):
        part = at_cluster(r.rb2, t)[PAD : 2 * PAD]
        if t > 0:
            part = part + at_cluster(r.rb2, t - 1)[2 * PAD : 3 * PAD]
        if t < C - 1:
            part = part + at_cluster(r.rb2, t + 1)[0:PAD]
        parts.append(part)
    coarse_image = filled(jnp.concatenate(parts, axis=0))
    shift = solve(coarse_image)
    keep(2, shift)
    shift = filled(shift)
    near_shift = near(2, 0)
    columns = filled(r.cinv[pl.ds(PAD * c, 3 * PAD), :]).T[:, 0 : 3 * PAD]

    total = sub_total(r.ra3, 3)
    answers = jnp.dot(columns, total, precision=HIGHEST)
    tile_rows = lax.broadcasted_iota(jnp.int32, (PAD, 128), 0)
    for t in range(C):
        tile = answers[PAD * t : PAD * (t + 1)]
        r.ub3[t] = jnp.where(tile_rows < 6, tile, total[0:PAD])
    r.rb3[c] = r.ub3[c]
    cluster_start(lambda there: r.ub3.at[there], r.rb3, 3)

    bent = jnp.dot(gfg, shift, precision=HIGHEST)
    overlap = column_sum(coarse_image * shift)
    bent_energy = column_sum(bent * shift)
    shift_energy = 2.0 * column_sum(near_shift * total)

    r.sb[c] = sub_total(r.sa, 4) - shift_energy
    cluster_start(lambda there: r.sb.at[c], r.sb, 4)

    own_inverse = r.cinv[pl.ds(PAD * (c + 1), PAD), :]
    bent_own = jnp.dot(own_inverse, bent, precision=HIGHEST)
    shift_own = near_shift[PAD : 2 * PAD]
    first_own = near(1, 0)[PAD : 2 * PAD]
    weights = packed(near_shift)
    for f in range(4):
        r.y[f] = r.y[f] - spread(weights, f)
    out_w = pltpu.make_async_copy(r.y, r.w_hbm, r.osem.at[2])
    out_w.start()

    total = cluster_total(r.rb3, 3)
    curvature_now = total[7:8]
    length = norm_now / curvature_now
    w_square = total[6:7] - overlap
    w_energy = cluster_total(r.sb, 4) + bent_energy
    norm_next = length * length * w_square - norm_now
    ratio = norm_next / norm_now
    z_energy = curvature_now - 2.0 * length * w_square + length * length * w_energy
    zd_energy = curvature_now - length * w_square
    curvature_next = z_energy + 2.0 * ratio * zd_energy + ratio * ratio * curvature_now
    step = norm_next / curvature_next
    last = (
        first_own
        - length * shift_own
        - step * ((1.0 + ratio) * shift_own - length * (total - bent_own))
    )
    r.last_out[0:PAD] = last
    r.last_out[PAD : PAD + 1] = length + step * (1.0 + ratio)
    r.last_out[PAD + 1 : PAD + 2] = step * length

    for k, buf in enumerate([r.ka, r.ra0, r.ra2, r.ra3, r.sa]):
        wait_bytes(buf.at[pl.ds(0, S - 1)], r.asend.at[k])
    wait_bytes(r.eb.at[pl.ds(0, C - 1)], r.esend)
    for k, buf in ((0, r.kb), (3, r.rb3), (4, r.sb)):
        wait_bytes(buf.at[pl.ds(0, C - 1)], r.bsend.at[k])
    for k, buf in ((1, r.rb0), (2, r.rb2)):
        wait_bytes(buf.at[0, pl.ds(0, Z - 1)], r.bsend.at[k])
        wait_bytes(buf.at[0], r.ksend.at[k])
    for f in range(4):

        @pl.when(has[f])
        def _():
            halo_copy(r.load, 0, f).wait_send()
            halo_copy(r.im0, 1, f).wait_send()
            modes_copy(f).wait_send()

    out_lam.wait()
    out_z0.wait()
    out_w.wait()


def finish(sign, last, lam, z0, w, out, amp_out):
    f = pl.program_id(0)
    grow, back = last[PAD : PAD + 1], last[PAD + 1 : PAD + 2]
    for k in range(4):
        turned = sign[0, 0, 4 * k + f].astype(F32)
        out[k, 0] = turned * (lam[0, k] + grow * z0[0, k] - back * w[0, k])
    amp_out[:, 0] = last[:MODES]


def per_device(C, S, dual_ops, local_load, rigid_modes, coarse_load, gluing_peer, gluing_sign):
    size = dual_ops.shape[-1]
    block = size // 16
    loads = local_load.shape[-1]
    hbm = pl.BlockSpec(memory_space=pltpu.HBM)
    dma = pltpu.SemaphoreType.DMA
    field = pltpu.VMEM((4, 4, block, loads), F32)

    def rows(*shape):
        return pltpu.VMEM((*shape, 128), F32)

    scratch = dict(
        peer=pltpu.SMEM((1, 1, 16), jnp.int32),
        dual=pltpu.VMEM((4, 4, block, size), BF16),
        load=field,
        modes=pltpu.VMEM((MODES, 16, block), F32),
        cload=pltpu.VMEM((MODES, 1, loads), F32),
        lam=field,
        z0=field,
        y=field,
        im0=field,
        rhs=pltpu.VMEM((4, 4, block, 2 * loads), BF16),
        basis=pltpu.VMEM((4, 4, block, 384), BF16),
        t3=pltpu.VMEM((6 * PAD, size), BF16),
        d3=pltpu.VMEM((6 * PAD, size), BF16),
        cinv=rows(PAD * (C + 2)),
        coef=rows(3, PAD * (C + 4)),
        msg=rows(4, block),
        ka=rows(S, PAD),
        kb=rows(C, PAD),
        eb=rows(C, PAD),
        ra0=rows(S, 4 * PAD),
        rb0=rows(2, C // 2, 4 * PAD),
        ra2=rows(S, 3 * PAD),
        rb2=rows(2, C // 2, 3 * PAD),
        ra3=rows(S, 3 * PAD),
        ub3=rows(C, PAD),
        rb3=rows(C, PAD),
        sa=rows(S, 1),
        sb=rows(C, 1),
        lsem=dma((8,)),
        osem=dma((3,)),
        hsend=dma((2, 4)),
        hrecv=dma((2, 4)),
        gsend=dma((4,)),
        grecv=dma((4,)),
        asend=dma((5,)),
        arecv=dma((5,)),
        bsend=dma((5,)),
        brecv=dma((5,)),
        ksend=dma((4,)),
        krecv=dma((4,)),
        esend=dma,
        erecv=dma,
    )
    for f in range(4):
        scratch["h0%d" % f] = rows(4, block)
        scratch["h1%d" % f] = rows(4, block)
        scratch["a%d" % f] = rows(block)
        scratch["r%d" % f] = rows(4, block)
    whole = jax.ShapeDtypeStruct((4, 4, block, loads), F32)
    lam, z0, w, last = pl.pallas_call(
        functools.partial(kernel, C, S),
        out_shape=(whole, whole, whole, jax.ShapeDtypeStruct((2 * PAD, loads), F32)),
        in_specs=[hbm] * 5,
        out_specs=(hbm, hbm, hbm, pl.BlockSpec(memory_space=pltpu.VMEM)),
        scratch_shapes=[scratch[name] for name in NAMES[9:]],
        compiler_params=pltpu.CompilerParams(
            collective_id=0, has_side_effects=True, vmem_limit_bytes=56 * 1024 * 1024
        ),
    )(
        gluing_peer,
        dual_ops.reshape(4, 4, block, size),
        local_load.reshape(4, 4, block, loads),
        rigid_modes.reshape(MODES, 16, block),
        coarse_load.reshape(MODES, 1, loads),
    )
    face = pl.BlockSpec((1, 4, block, loads), lambda f: (f, 0, 0, 0))
    multipliers, amplitudes = pl.pallas_call(
        finish,
        grid=(4,),
        out_shape=(whole, jax.ShapeDtypeStruct((MODES, 1, loads), F32)),
        in_specs=[
            pl.BlockSpec(memory_space=pltpu.SMEM),
            pl.BlockSpec((2 * PAD, loads), lambda f: (0, 0)),
            face,
            face,
            face,
        ],
        out_specs=(
            pl.BlockSpec((4, 1, block, loads), lambda f: (0, f, 0, 0)),
            pl.BlockSpec((MODES, 1, loads), lambda f: (0, 0, 0)),
        ),
    )(gluing_sign, last, lam, z0, w)
    return multipliers.reshape(1, 1, size, loads), amplitudes.reshape(1, MODES, loads)


def solution(mesh):
    return jax.shard_map(
        functools.partial(per_device, mesh.shape["cluster"], mesh.shape["sub"]),
        mesh=mesh,
        in_specs=(
            P("cluster", "sub", None, None),
            P("cluster", "sub", None, None),
            P("cluster", "sub", None, None),
            P("cluster", None, None),
            P("cluster", "sub", None),
            P("cluster", "sub", None),
        ),
        out_specs=(P("cluster", "sub", None, None), P("cluster", None, None)),
        check_vma=False,
    )
```

```python
import functools
import types

import jax
import jax.numpy as jnp
from jax import lax
from jax.experimental import pallas as pl
from jax.experimental.pallas import tpu as pltpu
from jax.sharding import PartitionSpec as P

MESH = pl.DeviceIdType.MESH
HIGHEST = lax.Precision.HIGHEST
F32 = jnp.float32
BF16 = jnp.bfloat16
MODES = 6
PAD = 8


def split(value):
    high = value.astype(BF16)
    low = (value - high.astype(F32)).astype(BF16)
    return high, low


def elimination_levels(count):
    levels, step = [], 1
    while step < count:
        levels.append(list(range(step, count, 2 * step)))
        step *= 2
    return levels + [[0]]


def coarse_inverse(tiles):
    count = len(tiles)
    rows = lax.broadcasted_iota(jnp.int32, (PAD, 128), 0)
    lanes = lax.broadcasted_iota(jnp.int32, (PAD, 128), 1)
    left = list(tiles)
    right = [
        jnp.where((lanes == rows + PAD * t) & (rows < MODES), 1.0, 0.0).astype(F32)
        for t in range(count)
    ]
    pattern = [[abs(t - u) <= 1 for u in range(count)] for t in range(count)]
    scale = [jnp.ones((PAD, 128), F32) for _ in range(count)]
    for level in elimination_levels(count):
        touched = {p: [t for t in range(count) if pattern[t][p]] for p in level}
        for mode in range(MODES):
            updates = []
            for p in level:
                column = PAD * p + mode
                factors = {
                    t: jnp.broadcast_to(left[t][:, column : column + 1], (PAD, 128))
                    for t in touched[p]
                }
                inverse = 1.0 / factors[p][mode : mode + 1, :]
                row_left = left[p][mode : mode + 1, :] * inverse
                row_right = right[p][mode : mode + 1, :] * inverse
                factors[p] = jnp.where(rows == mode, 0.0, factors[p])
                scale[p] = jnp.where(rows == mode, inverse, scale[p])
                updates.append((factors, row_left, row_right))
            for factors, row_left, row_right in updates:
                for t, factor in factors.items():
                    left[t] = left[t] - factor * row_left
                    right[t] = right[t] - factor * row_right
        for p in level:
            for t in touched[p]:
                for u in range(count):
                    pattern[t][u] = pattern[t][u] or pattern[p][u]
    return [r * k for r, k in zip(right, scale)]


NAMES = (
    "peer_hbm",
    "dual_hbm",
    "load_hbm",
    "modes_hbm",
    "cload_hbm",
    "lam_hbm",
    "z0_hbm",
    "w_hbm",
    "last_out",
    "peer",
    "dual",
    "load",
    "modes",
    "cload",
    "lam",
    "z0",
    "y",
    "im0",
    "h00",
    "h01",
    "h02",
    "h03",
    "h10",
    "h11",
    "h12",
    "h13",
    "a0",
    "a1",
    "a2",
    "a3",
    "r0",
    "r1",
    "r2",
    "r3",
    "rhs",
    "basis",
    "t3",
    "d3",
    "cinv",
    "coef",
    "msg",
    "ka",
    "kb",
    "eb",
    "ra0",
    "rb0",
    "ra2",
    "rb2",
    "ra3",
    "ub3",
    "rb3",
    "sa",
    "sb",
    "lsem",
    "dsem",
    "osem",
    "hsend",
    "hrecv",
    "gsend",
    "grecv",
    "asend",
    "arecv",
    "bsend",
    "brecv",
    "zsend",
    "zrecv",
    "ksend",
    "krecv",
    "esend",
    "erecv",
)


def kernel(C, S, *refs):
    r = types.SimpleNamespace(**dict(zip(NAMES, refs)))
    c = lax.axis_index("cluster")
    s = lax.axis_index("sub")
    Z = C // 2
    z, core = c // 2, lax.rem(c, 2)
    has = [s > 0, s < S - 1, c > 0, c < C - 1]
    towards = [(c, s - 1), (c, s + 1), (c - 1, s), (c + 1, s)]
    halo = [[r.h00, r.h01, r.h02, r.h03], [r.h10, r.h11, r.h12, r.h13]]
    near_modes = [r.a0, r.a1, r.a2, r.a3]
    turned_modes = [r.r0, r.r1, r.r2, r.r3]
    size = r.dual.shape[3]

    cp_modes = pltpu.make_async_copy(r.modes_hbm, r.modes, r.lsem.at[0])
    cp_cload = pltpu.make_async_copy(r.cload_hbm, r.cload, r.lsem.at[1])
    cp_dual = pltpu.make_async_copy(r.dual_hbm, r.dual, r.dsem)
    cp_load = [
        pltpu.make_async_copy(r.load_hbm.at[:, f], r.load.at[f], r.lsem.at[3 + f]) for f in range(4)
    ]
    cp_peer = pltpu.make_async_copy(r.peer_hbm, r.peer, r.lsem.at[7])
    cp_modes.start()
    cp_peer.start()
    cp_cload.start()
    for copy in cp_load:
        copy.start()
    cp_dual.start()

    barrier = pltpu.get_barrier_semaphore()

    def greet_sub(i, carry):
        pl.semaphore_signal(
            barrier, inc=1, device_id=(c, lax.rem(s + i, S)), device_id_type=MESH
        )
        return carry

    def greet_cluster(i, carry):
        pl.semaphore_signal(
            barrier, inc=1, device_id=(lax.rem(c + i, C), s), device_id_type=MESH
        )
        return carry

    lax.fori_loop(1, S, greet_sub, 0)
    lax.fori_loop(1, C, greet_cluster, 0)

    def send(src, dst, send_sem, recv_sem, device):
        pltpu.make_async_remote_copy(
            src_ref=src,
            dst_ref=dst,
            send_sem=send_sem,
            recv_sem=recv_sem,
            device_id=device,
            device_id_type=MESH,
        ).start()

    def wait_bytes(part, sem):
        pltpu.make_async_copy(part, part, sem).wait()

    def sub_start(buf, k):
        def body(i, carry):
            send(buf.at[s], buf.at[s], r.asend.at[k], r.arecv.at[k], (c, lax.rem(s + i, S)))
            return carry

        lax.fori_loop(1, S, body, 0)

    def sub_total(buf, k):
        wait_bytes(buf.at[pl.ds(0, S - 1)], r.arecv.at[k])
        total = buf[0]
        for i in range(1, S):
            total = total + buf[i]
        return total

    def chips_start(buf, k):
        def body(i, carry):
            there = lax.rem(z + i, Z) * 2 + core
            send(buf.at[core, z], buf.at[core, z], r.zsend.at[k], r.zrecv.at[k, z], (there, s))
            return carry

        lax.fori_loop(1, Z, body, 0)
        pass_on(buf, k, z)

    def pass_on(buf, k, row):
        part = buf.at[core, row]
        send(part, part, r.ksend.at[k], r.krecv.at[k], (2 * z + 1 - core, s))

    def chips_end(buf, k):
        for i in sorted(range(1, Z), key=lambda i: min(i, Z - i)):
            row = lax.rem(z + i, Z)
            wait_bytes(buf.at[core, row], r.zrecv.at[k, row])
            pass_on(buf, k, row)

    def cores_end(buf, k):
        wait_bytes(buf.at[0], r.krecv.at[k])

    def cluster_start(src, buf, k):
        def body(i, carry):
            there = lax.rem(c + i, C)
            send(src(there), buf.at[c], r.bsend.at[k], r.brecv.at[k], (there, s))
            return carry

        lax.fori_loop(1, C, body, 0)

    def cluster_wait(buf, k):
        wait_bytes(buf.at[pl.ds(0, C - 1)], r.brecv.at[k])

    def cluster_total(buf, k):
        cluster_wait(buf, k)
        total = buf[0]
        for t in range(1, C):
            total = total + buf[t]
        return total

    def halo_copy(src, x, f):
        return pltpu.make_async_remote_copy(
            src_ref=src.at[f],
            dst_ref=halo[x][f ^ 1],
            send_sem=r.hsend.at[x, f],
            recv_sem=r.hrecv.at[x, f ^ 1],
            device_id=towards[f],
            device_id_type=MESH,
        )

    def modes_copy(f):
        return pltpu.make_async_remote_copy(
            src_ref=r.msg.at[f],
            dst_ref=near_modes[f ^ 1],
            send_sem=r.gsend.at[f],
            recv_sem=r.grecv.at[f ^ 1],
            device_id=towards[f],
            device_id_type=MESH,
        )

    for f in range(4):

        @pl.when(jnp.logical_not(has[f]))
        def _():
            for x in range(2):
                halo[x][f][...] = jnp.zeros((4, 128, 128), F32)
            near_modes[f][...] = jnp.zeros((128, 128), F32)

    r.coef[...] = jnp.zeros(r.coef.shape, F32)

    cp_modes.wait()
    cp_peer.wait()
    rows = jnp.concatenate([r.modes[:, b] for b in range(16)], axis=1)
    rows = jnp.concatenate([rows, jnp.zeros((PAD - MODES, size), F32)], axis=0)
    face = (lax.broadcasted_iota(jnp.int32, (PAD, size), 1) // 128) % 4
    at_rim0 = jnp.where(s > 0, 0.0, 1.0)
    at_rim1 = jnp.where(s < S - 1, 0.0, 1.0)
    low_on = jnp.where(c > 0, 1.0, 0.0)
    high_on = jnp.where(c < C - 1, 1.0, 0.0)
    rows2 = jnp.where(face == 2, rows, 0.0)
    rows3 = jnp.where(face == 3, rows, 0.0)
    own = jnp.where(face >= 2, rows, jnp.where(face == 0, rows * at_rim0, rows * at_rim1))
    span = jnp.concatenate([-low_on * rows2, own, -high_on * rows3], axis=0)

    coarse_row = lax.dot_general(
        rows, span, (((1,), (1,)), ((), ())), precision=HIGHEST, preferred_element_type=F32
    )
    coarse_row = jnp.concatenate([coarse_row, jnp.zeros((PAD, 128 - 3 * PAD), F32)], axis=1)
    coarse_row = pltpu.roll(coarse_row, lax.rem(PAD * c + 128 - PAD, 128), 1)

    cp_cload.wait()
    r.eb[c] = jnp.concatenate(
        [r.cload[:, 0], jnp.zeros((PAD - MODES, 128), F32)], axis=0
    )

    by_face = [
        jnp.concatenate(
            [part[:, 128 * (4 * k + f) : 128 * (4 * k + f + 1)] for f in range(4) for k in range(4)],
            axis=1,
        )
        for part in (own, rows2, rows3)
    ]
    t3_high, t3_low = split(jnp.concatenate(by_face, axis=0))
    r.t3[...] = jnp.concatenate([t3_high, t3_low], axis=0)
    def rows_times(left, high, low):
        pair = jnp.dot(
            left[...], jnp.concatenate([high, low], axis=1), preferred_element_type=F32
        )
        half = 3 * PAD
        return pair[:half, :128] + (pair[half:, :128] + pair[:half, 128:]) + pair[half:, 128:]

    def field_terms(left, field):
        return rows_times(left, *split(field[...].reshape(size, 128)))

    for copy in cp_load:
        copy.wait()
    load_terms = field_terms(r.t3, r.load)
    r.ra0[s] = jnp.concatenate(
        [load_terms[PAD * kind : PAD * kind + MODES] for kind in range(3)] + [coarse_row[0:MODES]],
        axis=0,
    )

    turned = []

    def mode_images(f):
        if f == 0:
            cp_dual.wait()
        part = jnp.dot(
            r.dual[:, f].reshape(size // 4, size),
            r.basis[:, :, :, 256:384].reshape(size, 128),
            preferred_element_type=F32,
        ).reshape(4, 128, 128)
        side = None
        for k in range(4):
            block = jnp.where(lanes < 3 * PAD, part[k] + pltpu.roll(part[k], 96, 1), 0.0)
            r.im0[f, k] = block
            turned.append(block.T[0 : 3 * PAD])
            r.basis[k, f, :, 0:128] = tripled(block)
            side = block if side is None else side + pltpu.roll(block, 32 * k, 1)
        r.msg[f] = side

    pl.semaphore_wait(barrier, S - 1 + C - 1)
    sub_start(r.ra0, 1)

    def send_e(i, carry):
        send(r.eb.at[c], r.eb.at[c], r.esend, r.erecv, (lax.rem(c + i, C), s))
        return carry

    lax.fori_loop(1, C, send_e, 0)

    span_high = span.astype(BF16).astype(F32)
    gap = jnp.zeros((PAD, size), F32)
    wide = jnp.concatenate(
        [span_high, gap, span - span_high, gap, span_high, gap, gap, gap, gap, gap], axis=0
    )
    for b in range(16):
        r.basis[b // 4, b % 4, :, 256:384] = wide[:, 128 * b : 128 * (b + 1)].T.astype(BF16)

    lanes = lax.broadcasted_iota(jnp.int32, (128, 128), 1)

    def tripled(value):
        high = value.astype(BF16).astype(F32)
        return (high + pltpu.roll(value - high, 32, 1) + pltpu.roll(high, 64, 1)).astype(BF16)

    for f in range(4):
        mode_images(f)
    d3_high, d3_low = split(jnp.concatenate(turned, axis=1))
    r.d3[...] = jnp.concatenate([d3_high, d3_low], axis=0)
    mode_terms = field_terms(r.t3, r.im0)
    r.ka[s] = (
        mode_terms[0:PAD]
        + pltpu.roll(mode_terms[PAD : 2 * PAD], 32, 1)
        + pltpu.roll(mode_terms[2 * PAD : 3 * PAD], 64, 1)
    )
    sub_start(r.ka, 0)
    r.rb0[core, z] = sub_total(r.ra0, 1)
    chips_start(r.rb0, 0)
    r.kb[c] = sub_total(r.ka, 0)
    cluster_start(lambda there: r.kb.at[c], r.kb, 0)

    for f in range(4):

        @pl.when(has[f])
        def _():
            halo_copy(r.load, 0, f).start()
            modes_copy(f).start()

    chips_end(r.rb0, 0)
    cores_end(r.rb0, 0)
    blank = jnp.zeros((PAD - MODES, 128), F32)
    inverse = coarse_inverse(
        [
            jnp.concatenate([r.rb0[t % 2, t // 2, 3 * MODES : 4 * MODES], blank], axis=0)
            for t in range(C)
        ]
    )
    zero_tile = jnp.zeros((PAD, 128), F32)
    r.cinv[0:PAD] = zero_tile
    for t in range(C):
        r.cinv[PAD * (t + 1) : PAD * (t + 2)] = inverse[t]
    r.cinv[PAD * (C + 1) : PAD * (C + 2)] = zero_tile

    def filled(value):
        if value.shape[0] < 128:
            value = jnp.concatenate([value, jnp.zeros((128 - value.shape[0], 128), F32)], axis=0)
        return value

    def solve(right):
        return jnp.dot(r.cinv[PAD : PAD * (C + 1), :], right, precision=HIGHEST)

    def keep(k, value):
        r.coef[k, 2 * PAD : PAD * (C + 2)] = value

    def near(k, offset):
        return r.coef[k, pl.ds(PAD * (c + 1 + offset), 3 * PAD), :]

    def packed(value):
        high = value.astype(BF16).astype(F32)
        empty = jnp.zeros((PAD, 128), F32)
        return jnp.concatenate(
            [high, empty, high, empty, value - high, empty, empty, empty, empty, empty], axis=0
        ).astype(BF16)

    wait_bytes(r.eb.at[pl.ds(0, C - 1)], r.erecv)
    start = solve(filled(jnp.concatenate([r.eb[t] for t in range(C)], axis=0)))
    keep(0, start)
    start = filled(start)

    for f in range(4):

        @pl.when(has[f])
        def _():
            wait_bytes(halo[0][f], r.hrecv.at[0, f])
            wait_bytes(near_modes[f], r.grecv.at[f])

    start_here = packed(near(0, 0))
    start_near = [start_here, start_here, packed(near(0, -1)), packed(near(0, 1))]
    for f in range(4):
        for j in range(4):
            group = r_f = near_modes[f][...]
            if j:
                group = pltpu.roll(r_f, 128 - 32 * j, 1)
            turned_modes[f][j] = jnp.where(lanes < 3 * PAD, group, 0.0)
        for k in range(4):
            r.basis[k, f, :, 128:256] = tripled(turned_modes[f][r.peer[0, 0, 4 * k + f]])
        image = jnp.dot(
            r.basis[:, f, :, 0:256].reshape(size // 4, 256),
            jnp.concatenate([start_here, -start_near[f]], axis=0),
            preferred_element_type=F32,
        ).reshape(4, 128, 128)
        spread_start = jnp.dot(
            r.basis[:, f, :, 256:384].reshape(size // 4, 128),
            start_here,
            preferred_element_type=F32,
        ).reshape(4, 128, 128)
        r.lam[f] = spread_start
        for k in range(4):
            r.z0[f, k] = r.load[f, k] - halo[0][f][r.peer[0, 0, 4 * k + f]] - image[k]

    out_lam = pltpu.make_async_copy(r.lam, r.lam_hbm, r.osem.at[0])
    out_lam.start()

    def joined(tile):
        parts = []
        for t in range(C):
            part = tile(t, 0)
            if t > 0:
                part = part - tile(t - 1, 2)
            if t < C - 1:
                part = part - tile(t + 1, 1)
            parts += [part, blank]
        return filled(jnp.concatenate(parts, axis=0))

    def load_term(t, kind):
        return r.rb0[t % 2, t // 2, MODES * kind : MODES * (kind + 1)]

    tile_lanes = lax.broadcasted_iota(jnp.int32, (MODES, 128), 1)

    def mode_term(t, kind):
        value = r.kb[t, 0:MODES]
        value = jnp.where((tile_lanes >= 32 * kind) & (tile_lanes < 32 * kind + 3 * PAD), value, 0.0)
        turn = (PAD * (t - 1) - 32 * kind) % 128
        return pltpu.roll(value, turn, 1) if turn else value

    cluster_wait(r.kb, 0)
    gfg = joined(mode_term)
    coarse_now = joined(load_term) - jnp.dot(gfg, start, precision=HIGHEST)
    first = solve(coarse_now)
    keep(1, first)
    weights = packed(near(1, 0))

    half_on = [jnp.where(has[f], 0.5, 1.0) for f in range(4)]

    def folded(value):
        return jnp.sum(value.reshape(-1, PAD, 128), axis=0)

    def column_sum(parts):
        return jnp.sum(parts, axis=0, keepdims=True)

    def spread(weights, f):
        return jnp.dot(
            r.basis[:, f, :, 256:384].reshape(size // 4, 128), weights, preferred_element_type=F32
        ).reshape(4, 128, 128)

    row_ids = lax.broadcasted_iota(jnp.int32, (3 * PAD, 128), 0)

    def with_rows(terms, scalars):
        for row, value in scalars:
            terms = jnp.where(row_ids == row, value, terms)
        return terms

    norm = jnp.zeros((PAD, 128), F32)
    for f in range(4):
        value = r.z0[f] - spread(weights, f)
        r.z0[f] = value
        r.rhs[:, f, :, 0:128] = value.astype(BF16)
        norm = norm + half_on[f] * folded(value * value)
    out_z0 = pltpu.make_async_copy(r.z0, r.z0_hbm, r.osem.at[1])
    out_z0.start()
    r.ra2[s] = with_rows(field_terms(r.d3, r.z0), [(6, column_sum(norm))])
    sub_start(r.ra2, 2)

    for f in range(4):
        r.im0[f] = jnp.dot(
            r.dual[:, f].reshape(size // 4, size),
            r.rhs[:, :, :, 0:128].reshape(size, 128),
            preferred_element_type=F32,
        ).reshape(4, 128, 128)

        @pl.when(has[f])
        def _():
            halo_copy(r.im0, 1, f).start()

    columns = filled(r.cinv[pl.ds(PAD * c, 3 * PAD), :]).T[:, 0 : 3 * PAD]
    own_inverse = r.cinv[pl.ds(PAD * (c + 1), PAD), :]
    r.rb2[core, z] = sub_total(r.ra2, 2)
    chips_start(r.rb2, 1)

    for f in range(4):

        @pl.when(has[f])
        def _():
            wait_bytes(halo[1][f], r.hrecv.at[1, f])

    square = jnp.zeros((PAD, 128), F32)
    cross = jnp.zeros((PAD, 128), F32)
    for f in range(4):
        for k in range(4):
            value = r.im0[f, k] - halo[1][f][r.peer[0, 0, 4 * k + f]]
            r.y[f, k] = value
            high, low = split(value)
            r.rhs[k, f, :, 0:128] = high
            r.rhs[k, f, :, 128:256] = low
            square = square + half_on[f] * folded(value * value)
            cross = cross + half_on[f] * folded(value * r.z0[f, k])
    r.ra3[s] = with_rows(
        field_terms(r.d3, r.y), [(6, column_sum(square)), (7, column_sum(cross))]
    )
    sub_start(r.ra3, 3)

    energy = jnp.zeros((PAD, 128), F32)
    for f in range(4):
        pair = jnp.dot(
            r.dual[:, f].reshape(size // 4, size),
            r.rhs[...].reshape(size, 256),
            preferred_element_type=F32,
        )
        part = (pair[:, :128] + pair[:, 128:]).reshape(4, 128, 128)
        energy = energy + folded(r.y[f] * part)
        if f == 1:
            chips_end(r.rb2, 1)
    r.sa[s] = column_sum(energy)
    sub_start(r.sa, 4)

    cores_end(r.rb2, 1)
    norm_now = r.rb2[0, 0, 6:7]
    for t in range(1, C):
        norm_now = norm_now + r.rb2[t % 2, t // 2, 6:7]
    parts = []
    for t in range(C):
        part = r.rb2[t % 2, t // 2, PAD : 2 * PAD]
        if t > 0:
            part = part + r.rb2[(t - 1) % 2, (t - 1) // 2, 2 * PAD : 3 * PAD]
        if t < C - 1:
            part = part + r.rb2[(t + 1) % 2, (t + 1) // 2, 0:PAD]
        parts.append(part)
    coarse_image = filled(jnp.concatenate(parts, axis=0))
    shift = solve(coarse_image)
    keep(2, shift)
    shift = filled(shift)
    near_shift = near(2, 0)

    total = sub_total(r.ra3, 3)
    answers = jnp.dot(columns, total, precision=HIGHEST)
    tile_rows = lax.broadcasted_iota(jnp.int32, (PAD, 128), 0)
    for t in range(C):
        tile = answers[PAD * t : PAD * (t + 1)]
        r.ub3[t] = jnp.where(tile_rows < 6, tile, total[0:PAD])
    r.rb3[c] = r.ub3[c]
    cluster_start(lambda there: r.ub3.at[there], r.rb3, 3)

    bent = jnp.dot(gfg, shift, precision=HIGHEST)
    overlap = column_sum(coarse_image * shift)
    bent_energy = column_sum(bent * shift)
    shift_energy = 2.0 * column_sum(near_shift * total)

    r.sb[c] = sub_total(r.sa, 4) - shift_energy
    cluster_start(lambda there: r.sb.at[c], r.sb, 4)

    bent_own = jnp.dot(own_inverse, bent, precision=HIGHEST)
    shift_own = near_shift[PAD : 2 * PAD]
    first_own = near(1, 0)[PAD : 2 * PAD]
    weights = packed(near_shift)
    for f in range(4):
        r.y[f] = r.y[f] - spread(weights, f)
    out_w = pltpu.make_async_copy(r.y, r.w_hbm, r.osem.at[2])
    out_w.start()

    total = cluster_total(r.rb3, 3)
    curvature_now = total[7:8]
    length = norm_now / curvature_now
    w_square = total[6:7] - overlap
    w_energy = cluster_total(r.sb, 4) + bent_energy
    norm_next = length * length * w_square - norm_now
    ratio = norm_next / norm_now
    z_energy = curvature_now - 2.0 * length * w_square + length * length * w_energy
    zd_energy = curvature_now - length * w_square
    curvature_next = z_energy + 2.0 * ratio * zd_energy + ratio * ratio * curvature_now
    step = norm_next / curvature_next
    last = (
        first_own
        - length * shift_own
        - step * ((1.0 + ratio) * shift_own - length * (total - bent_own))
    )
    r.last_out[0:PAD] = last
    r.last_out[PAD : PAD + 1] = length + step * (1.0 + ratio)
    r.last_out[PAD + 1 : PAD + 2] = step * length

    for k, buf in enumerate([r.ka, r.ra0, r.ra2, r.ra3, r.sa]):
        wait_bytes(buf.at[pl.ds(0, S - 1)], r.asend.at[k])
    wait_bytes(r.eb.at[pl.ds(0, C - 1)], r.esend)
    for k, buf in enumerate([r.rb0, r.rb2]):
        wait_bytes(buf.at[0, pl.ds(0, Z - 1)], r.zsend.at[k])
        wait_bytes(buf.at[0], r.ksend.at[k])
    for k, buf in ((0, r.kb), (3, r.rb3), (4, r.sb)):
        wait_bytes(buf.at[pl.ds(0, C - 1)], r.bsend.at[k])
    for f in range(4):

        @pl.when(has[f])
        def _():
            halo_copy(r.load, 0, f).wait_send()
            halo_copy(r.im0, 1, f).wait_send()
            modes_copy(f).wait_send()

    out_lam.wait()
    out_z0.wait()
    out_w.wait()


def finish(sign, last_hbm, lam_hbm, z0_hbm, w_hbm, out_hbm, amp_hbm, last, lam, z0, w, amp, sems):
    cp_last = pltpu.make_async_copy(last_hbm, last, sems.at[4, 0])
    cp_last.start()
    copies = [
        [
            pltpu.make_async_copy(src.at[f], dst.at[f], sems.at[f, i])
            for i, (src, dst) in enumerate(((lam_hbm, lam), (z0_hbm, z0), (w_hbm, w)))
        ]
        for f in range(4)
    ]
    for group in copies:
        for copy in group:
            copy.start()
    cp_last.wait()
    grow, back = last[PAD : PAD + 1], last[PAD + 1 : PAD + 2]
    amp[:, 0] = last[:MODES]
    results = [pltpu.make_async_copy(amp, amp_hbm, sems.at[4, 1])]
    results[0].start()
    for f in range(4):
        for copy in copies[f]:
            copy.wait()
        for k in range(4):
            turned = sign[0, 0, 4 * k + f].astype(F32)
            lam[f, k] = turned * (lam[f, k] + grow * z0[f, k] - back * w[f, k])
        for k in range(4):
            result = pltpu.make_async_copy(lam.at[f, k], out_hbm.at[k, f], sems.at[5 + f, k])
            result.start()
            results.append(result)
    for result in results:
        result.wait()


def per_device(C, S, dual_ops, local_load, rigid_modes, coarse_load, gluing_peer, gluing_sign):
    size = dual_ops.shape[-1]
    block = size // 16
    loads = local_load.shape[-1]
    hbm = pl.BlockSpec(memory_space=pltpu.HBM)
    dma = pltpu.SemaphoreType.DMA
    field = pltpu.VMEM((4, 4, block, loads), F32)

    def rows(*shape):
        return pltpu.VMEM((*shape, 128), F32)

    scratch = dict(
        peer=pltpu.SMEM((1, 1, 16), jnp.int32),
        dual=pltpu.VMEM((4, 4, block, size), BF16),
        load=field,
        modes=pltpu.VMEM((MODES, 16, block), F32),
        cload=pltpu.VMEM((MODES, 1, loads), F32),
        lam=field,
        z0=field,
        y=field,
        im0=field,
        rhs=pltpu.VMEM((4, 4, block, 2 * loads), BF16),
        basis=pltpu.VMEM((4, 4, block, 384), BF16),
        t3=pltpu.VMEM((6 * PAD, size), BF16),
        d3=pltpu.VMEM((6 * PAD, size), BF16),
        cinv=rows(PAD * (C + 2)),
        coef=rows(3, PAD * (C + 4)),
        msg=rows(4, block),
        ka=rows(S, PAD),
        kb=rows(C, PAD),
        eb=rows(C, PAD),
        ra0=rows(S, 4 * MODES),
        rb0=rows(2, C // 2, 4 * MODES),
        ra2=rows(S, 3 * PAD),
        rb2=rows(2, C // 2, 3 * PAD),
        ra3=rows(S, 3 * PAD),
        ub3=rows(C, PAD),
        rb3=rows(C, PAD),
        sa=rows(S, 1),
        sb=rows(C, 1),
        lsem=dma((8,)),
        dsem=dma,
        osem=dma((3,)),
        hsend=dma((2, 4)),
        hrecv=dma((2, 4)),
        gsend=dma((4,)),
        grecv=dma((4,)),
        asend=dma((5,)),
        arecv=dma((5,)),
        bsend=dma((5,)),
        brecv=dma((5,)),
        zsend=dma((2,)),
        zrecv=dma((2, C // 2)),
        ksend=dma((2,)),
        krecv=dma((2,)),
        esend=dma,
        erecv=dma,
    )
    for f in range(4):
        scratch["h0%d" % f] = rows(4, block)
        scratch["h1%d" % f] = rows(4, block)
        scratch["a%d" % f] = rows(block)
        scratch["r%d" % f] = rows(4, block)
    whole = jax.ShapeDtypeStruct((4, 4, block, loads), F32)
    lam, z0, w, last = pl.pallas_call(
        functools.partial(kernel, C, S),
        out_shape=(whole, whole, whole, jax.ShapeDtypeStruct((2 * PAD, loads), F32)),
        in_specs=[hbm] * 5,
        out_specs=(hbm, hbm, hbm, pl.BlockSpec(memory_space=pltpu.VMEM)),
        scratch_shapes=[scratch[name] for name in NAMES[9:]],
        compiler_params=pltpu.CompilerParams(
            collective_id=0, has_side_effects=True, vmem_limit_bytes=56 * 1024 * 1024
        ),
    )(
        gluing_peer,
        dual_ops.reshape(4, 4, block, size),
        local_load.reshape(4, 4, block, loads),
        rigid_modes.reshape(MODES, 16, block),
        coarse_load.reshape(MODES, 1, loads),
    )
    multipliers, amplitudes = pl.pallas_call(
        finish,
        out_shape=(whole, jax.ShapeDtypeStruct((MODES, 1, loads), F32)),
        in_specs=[pl.BlockSpec(memory_space=pltpu.SMEM)] + [hbm] * 4,
        out_specs=(hbm, hbm),
        scratch_shapes=[
            rows(2 * PAD),
            field,
            field,
            field,
            pltpu.VMEM((MODES, 1, loads), F32),
            dma((9, 4)),
        ],
    )(gluing_sign, last, lam, z0, w)
    return multipliers.reshape(1, 1, size, loads), amplitudes.reshape(1, MODES, loads)


def solution(mesh):
    return jax.shard_map(
        functools.partial(per_device, mesh.shape["cluster"], mesh.shape["sub"]),
        mesh=mesh,
        in_specs=(
            P("cluster", "sub", None, None),
            P("cluster", "sub", None, None),
            P("cluster", "sub", None, None),
            P("cluster", None, None),
            P("cluster", "sub", None),
            P("cluster", "sub", None),
        ),
        out_specs=(P("cluster", "sub", None, None), P("cluster", None, None)),
        check_vma=False,
    )
```

```python
import functools
import types

import jax
import jax.numpy as jnp
from jax import lax
from jax.experimental import pallas as pl
from jax.experimental.pallas import tpu as pltpu
from jax.sharding import PartitionSpec as P

MESH = pl.DeviceIdType.MESH
HIGHEST = lax.Precision.HIGHEST
F32 = jnp.float32
BF16 = jnp.bfloat16
MODES = 6
PAD = 8


def split(value):
    high = value.astype(BF16)
    low = (value - high.astype(F32)).astype(BF16)
    return high, low


def elimination_levels(count):
    levels, step = [], 1
    while step < count:
        levels.append(list(range(step, count, 2 * step)))
        step *= 2
    return levels + [[0]]


def coarse_inverse(tiles):
    count = len(tiles)
    rows = lax.broadcasted_iota(jnp.int32, (PAD, 128), 0)
    lanes = lax.broadcasted_iota(jnp.int32, (PAD, 128), 1)
    left = list(tiles)
    right = [
        jnp.where((lanes == rows + PAD * t) & (rows < MODES), 1.0, 0.0).astype(F32)
        for t in range(count)
    ]
    pattern = [[abs(t - u) <= 1 for u in range(count)] for t in range(count)]
    scale = [jnp.ones((PAD, 128), F32) for _ in range(count)]
    for level in elimination_levels(count):
        touched = {p: [t for t in range(count) if pattern[t][p]] for p in level}
        for mode in range(MODES):
            updates = []
            for p in level:
                column = PAD * p + mode
                factors = {
                    t: jnp.broadcast_to(left[t][:, column : column + 1], (PAD, 128))
                    for t in touched[p]
                }
                inverse = 1.0 / factors[p][mode : mode + 1, :]
                row_left = left[p][mode : mode + 1, :] * inverse
                row_right = right[p][mode : mode + 1, :] * inverse
                factors[p] = jnp.where(rows == mode, 0.0, factors[p])
                scale[p] = jnp.where(rows == mode, inverse, scale[p])
                updates.append((factors, row_left, row_right))
            for factors, row_left, row_right in updates:
                for t, factor in factors.items():
                    left[t] = left[t] - factor * row_left
                    right[t] = right[t] - factor * row_right
        for p in level:
            for t in touched[p]:
                for u in range(count):
                    pattern[t][u] = pattern[t][u] or pattern[p][u]
    return [r * k for r, k in zip(right, scale)]


NAMES = (
    "peer_hbm",
    "dual_hbm",
    "load_hbm",
    "modes_hbm",
    "cload_hbm",
    "lam_hbm",
    "z0_hbm",
    "w_hbm",
    "last_out",
    "peer",
    "dual",
    "load",
    "modes",
    "cload",
    "lam",
    "z0",
    "y",
    "im0",
    "h00",
    "h01",
    "h02",
    "h03",
    "h10",
    "h11",
    "h12",
    "h13",
    "a0",
    "a1",
    "a2",
    "a3",
    "r0",
    "r1",
    "r2",
    "r3",
    "rhs",
    "basis",
    "t3",
    "d3",
    "cinv",
    "coef",
    "msg",
    "ka",
    "kb",
    "eb",
    "ra0",
    "rb0",
    "ra2",
    "rb2",
    "ra3",
    "ub3",
    "rb3",
    "sa",
    "sb",
    "lsem",
    "dsem",
    "osem",
    "hsend",
    "hrecv",
    "gsend",
    "grecv",
    "asend",
    "arecv",
    "bsend",
    "brecv",
    "zsend",
    "zrecv",
    "ksend",
    "krecv",
    "esend",
    "erecv",
)


def kernel(C, S, *refs):
    r = types.SimpleNamespace(**dict(zip(NAMES, refs)))
    c = lax.axis_index("cluster")
    s = lax.axis_index("sub")
    Z = C // 2
    z, core = c // 2, lax.rem(c, 2)
    has = [s > 0, s < S - 1, c > 0, c < C - 1]
    towards = [(c, s - 1), (c, s + 1), (c - 1, s), (c + 1, s)]
    halo = [[r.h00, r.h01, r.h02, r.h03], [r.h10, r.h11, r.h12, r.h13]]
    near_modes = [r.a0, r.a1, r.a2, r.a3]
    turned_modes = [r.r0, r.r1, r.r2, r.r3]
    size = r.dual.shape[3]

    cp_modes = pltpu.make_async_copy(r.modes_hbm, r.modes, r.lsem.at[0])
    cp_cload = pltpu.make_async_copy(r.cload_hbm, r.cload, r.lsem.at[1])
    cp_dual = pltpu.make_async_copy(r.dual_hbm, r.dual, r.dsem)
    cp_load = [
        pltpu.make_async_copy(r.load_hbm.at[:, f], r.load.at[f], r.lsem.at[3 + f]) for f in range(4)
    ]
    cp_peer = pltpu.make_async_copy(r.peer_hbm, r.peer, r.lsem.at[7])
    cp_modes.start()
    cp_peer.start()
    cp_cload.start()
    for copy in cp_load:
        copy.start()
    cp_dual.start()

    barrier = pltpu.get_barrier_semaphore()

    def greet_sub(i, carry):
        pl.semaphore_signal(
            barrier, inc=1, device_id=(c, lax.rem(s + i, S)), device_id_type=MESH
        )
        return carry

    def greet_cluster(i, carry):
        pl.semaphore_signal(
            barrier, inc=1, device_id=(lax.rem(c + i, C), s), device_id_type=MESH
        )
        return carry

    lax.fori_loop(1, S, greet_sub, 0)
    lax.fori_loop(1, C, greet_cluster, 0)

    def send(src, dst, send_sem, recv_sem, device):
        pltpu.make_async_remote_copy(
            src_ref=src,
            dst_ref=dst,
            send_sem=send_sem,
            recv_sem=recv_sem,
            device_id=device,
            device_id_type=MESH,
        ).start()

    def wait_bytes(part, sem):
        pltpu.make_async_copy(part, part, sem).wait()

    def sub_start(buf, k):
        def body(i, carry):
            send(buf.at[s], buf.at[s], r.asend.at[k], r.arecv.at[k], (c, lax.rem(s + i, S)))
            return carry

        lax.fori_loop(1, S, body, 0)

    def sub_total(buf, k):
        wait_bytes(buf.at[pl.ds(0, S - 1)], r.arecv.at[k])
        total = buf[0]
        for i in range(1, S):
            total = total + buf[i]
        return total

    def chips_start(buf, k):
        def body(i, carry):
            there = lax.rem(z + i, Z) * 2 + core
            send(buf.at[core, z], buf.at[core, z], r.zsend.at[k], r.zrecv.at[k, z], (there, s))
            return carry

        lax.fori_loop(1, Z, body, 0)
        pass_on(buf, k, z)

    def pass_on(buf, k, row):
        part = buf.at[core, row]
        send(part, part, r.ksend.at[k], r.krecv.at[k], (2 * z + 1 - core, s))

    def chips_end(buf, k):
        for i in sorted(range(1, Z), key=lambda i: min(i, Z - i)):
            row = lax.rem(z + i, Z)
            wait_bytes(buf.at[core, row], r.zrecv.at[k, row])
            pass_on(buf, k, row)

    def cores_end(buf, k):
        wait_bytes(buf.at[0], r.krecv.at[k])

    def cluster_start(src, buf, k):
        def body(i, carry):
            there = lax.rem(c + i, C)
            send(src(there), buf.at[c], r.bsend.at[k], r.brecv.at[k], (there, s))
            return carry

        lax.fori_loop(1, C, body, 0)

    def cluster_wait(buf, k):
        wait_bytes(buf.at[pl.ds(0, C - 1)], r.brecv.at[k])

    def cluster_total(buf, k):
        cluster_wait(buf, k)
        total = buf[0]
        for t in range(1, C):
            total = total + buf[t]
        return total

    def halo_copy(src, x, f):
        return pltpu.make_async_remote_copy(
            src_ref=src.at[f],
            dst_ref=halo[x][f ^ 1],
            send_sem=r.hsend.at[x, f],
            recv_sem=r.hrecv.at[x, f ^ 1],
            device_id=towards[f],
            device_id_type=MESH,
        )

    def modes_copy(f):
        return pltpu.make_async_remote_copy(
            src_ref=r.msg.at[f],
            dst_ref=near_modes[f ^ 1],
            send_sem=r.gsend.at[f],
            recv_sem=r.grecv.at[f ^ 1],
            device_id=towards[f],
            device_id_type=MESH,
        )

    for f in range(4):

        @pl.when(jnp.logical_not(has[f]))
        def _():
            for x in range(2):
                halo[x][f][...] = jnp.zeros((4, 128, 128), F32)
            near_modes[f][...] = jnp.zeros((128, 128), F32)

    r.coef[...] = jnp.zeros(r.coef.shape, F32)

    cp_modes.wait()
    cp_peer.wait()
    rows = jnp.concatenate([r.modes[:, b] for b in range(16)], axis=1)
    rows = jnp.concatenate([rows, jnp.zeros((PAD - MODES, size), F32)], axis=0)
    face = (lax.broadcasted_iota(jnp.int32, (PAD, size), 1) // 128) % 4
    at_rim0 = jnp.where(s > 0, 0.0, 1.0)
    at_rim1 = jnp.where(s < S - 1, 0.0, 1.0)
    low_on = jnp.where(c > 0, 1.0, 0.0)
    high_on = jnp.where(c < C - 1, 1.0, 0.0)
    rows2 = jnp.where(face == 2, rows, 0.0)
    rows3 = jnp.where(face == 3, rows, 0.0)
    own = jnp.where(face >= 2, rows, jnp.where(face == 0, rows * at_rim0, rows * at_rim1))
    span = jnp.concatenate([-low_on * rows2, own, -high_on * rows3], axis=0)

    coarse_row = lax.dot_general(
        rows, span, (((1,), (1,)), ((), ())), precision=HIGHEST, preferred_element_type=F32
    )
    coarse_row = jnp.concatenate([coarse_row, jnp.zeros((PAD, 128 - 3 * PAD), F32)], axis=1)
    coarse_row = pltpu.roll(coarse_row, lax.rem(PAD * c + 128 - PAD, 128), 1)

    cp_cload.wait()
    r.eb[c] = jnp.concatenate(
        [r.cload[:, 0], jnp.zeros((PAD - MODES, 128), F32)], axis=0
    )

    by_face = [
        jnp.concatenate(
            [part[:, 128 * (4 * k + f) : 128 * (4 * k + f + 1)] for f in range(4) for k in range(4)],
            axis=1,
        )
        for part in (own, rows2, rows3)
    ]
    t3_high, t3_low = split(jnp.concatenate(by_face, axis=0))
    r.t3[...] = jnp.concatenate([t3_high, t3_low], axis=0)
    def rows_times(left, high, low):
        pair = jnp.dot(
            left[...], jnp.concatenate([high, low], axis=1), preferred_element_type=F32
        )
        half = 3 * PAD
        return pair[:half, :128] + (pair[half:, :128] + pair[:half, 128:]) + pair[half:, 128:]

    def field_terms(left, field):
        return rows_times(left, *split(field[...].reshape(size, 128)))

    for copy in cp_load:
        copy.wait()
    load_terms = field_terms(r.t3, r.load)
    r.ra0[s] = jnp.concatenate(
        [load_terms[PAD * kind : PAD * kind + MODES] for kind in range(3)] + [coarse_row[0:MODES]],
        axis=0,
    )

    turned = []

    def mode_images(f):
        if f == 0:
            cp_dual.wait()
        part = jnp.dot(
            r.dual[:, f].reshape(size // 4, size),
            r.basis[:, :, :, 256:384].reshape(size, 128),
            preferred_element_type=F32,
        ).reshape(4, 128, 128)
        side = None
        for k in range(4):
            block = jnp.where(lanes < 3 * PAD, part[k] + pltpu.roll(part[k], 96, 1), 0.0)
            r.im0[f, k] = block
            turned.append(block.T[0 : 3 * PAD])
            r.basis[k, f, :, 0:128] = tripled(block)
            side = block if side is None else side + pltpu.roll(block, 32 * k, 1)
        r.msg[f] = side

    pl.semaphore_wait(barrier, S - 1 + C - 1)
    sub_start(r.ra0, 1)

    def send_e(i, carry):
        send(r.eb.at[c], r.eb.at[c], r.esend, r.erecv, (lax.rem(c + i, C), s))
        return carry

    lax.fori_loop(1, C, send_e, 0)

    span_high = span.astype(BF16).astype(F32)
    gap = jnp.zeros((PAD, size), F32)
    wide = jnp.concatenate(
        [span_high, gap, span - span_high, gap, span_high, gap, gap, gap, gap, gap], axis=0
    )
    for b in range(16):
        r.basis[b // 4, b % 4, :, 256:384] = wide[:, 128 * b : 128 * (b + 1)].T.astype(BF16)

    lanes = lax.broadcasted_iota(jnp.int32, (128, 128), 1)

    def tripled(value):
        high = value.astype(BF16).astype(F32)
        return (high + pltpu.roll(value - high, 32, 1) + pltpu.roll(high, 64, 1)).astype(BF16)

    for f in range(4):
        mode_images(f)
    d3_high, d3_low = split(jnp.concatenate(turned, axis=1))
    r.d3[...] = jnp.concatenate([d3_high, d3_low], axis=0)
    mode_terms = field_terms(r.t3, r.im0)
    r.ka[s] = (
        mode_terms[0:PAD]
        + pltpu.roll(mode_terms[PAD : 2 * PAD], 32, 1)
        + pltpu.roll(mode_terms[2 * PAD : 3 * PAD], 64, 1)
    )
    sub_start(r.ka, 0)
    r.rb0[core, z] = sub_total(r.ra0, 1)
    chips_start(r.rb0, 0)
    for f in range(4):

        @pl.when(has[f])
        def _():
            halo_copy(r.load, 0, f).start()
            modes_copy(f).start()

    r.kb[c] = sub_total(r.ka, 0)
    cluster_start(lambda there: r.kb.at[c], r.kb, 0)

    chips_end(r.rb0, 0)
    cores_end(r.rb0, 0)
    blank = jnp.zeros((PAD - MODES, 128), F32)
    inverse = coarse_inverse(
        [
            jnp.concatenate([r.rb0[t % 2, t // 2, 3 * MODES : 4 * MODES], blank], axis=0)
            for t in range(C)
        ]
    )
    zero_tile = jnp.zeros((PAD, 128), F32)
    r.cinv[0:PAD] = zero_tile
    for t in range(C):
        r.cinv[PAD * (t + 1) : PAD * (t + 2)] = inverse[t]
    r.cinv[PAD * (C + 1) : PAD * (C + 2)] = zero_tile

    def filled(value):
        if value.shape[0] < 128:
            value = jnp.concatenate([value, jnp.zeros((128 - value.shape[0], 128), F32)], axis=0)
        return value

    def solve(right):
        return jnp.dot(r.cinv[PAD : PAD * (C + 1), :], right, precision=HIGHEST)

    def keep(k, value):
        r.coef[k, 2 * PAD : PAD * (C + 2)] = value

    def near(k, offset):
        return r.coef[k, pl.ds(PAD * (c + 1 + offset), 3 * PAD), :]

    def packed(value):
        high = value.astype(BF16).astype(F32)
        empty = jnp.zeros((PAD, 128), F32)
        return jnp.concatenate(
            [high, empty, high, empty, value - high, empty, empty, empty, empty, empty], axis=0
        ).astype(BF16)

    wait_bytes(r.eb.at[pl.ds(0, C - 1)], r.erecv)
    start = solve(filled(jnp.concatenate([r.eb[t] for t in range(C)], axis=0)))
    keep(0, start)
    start = filled(start)

    for f in range(4):

        @pl.when(has[f])
        def _():
            wait_bytes(halo[0][f], r.hrecv.at[0, f])
            wait_bytes(near_modes[f], r.grecv.at[f])

    start_here = packed(near(0, 0))
    start_near = [start_here, start_here, packed(near(0, -1)), packed(near(0, 1))]
    for f in range(4):
        for j in range(4):
            group = r_f = near_modes[f][...]
            if j:
                group = pltpu.roll(r_f, 128 - 32 * j, 1)
            turned_modes[f][j] = jnp.where(lanes < 3 * PAD, group, 0.0)
        for k in range(4):
            r.basis[k, f, :, 128:256] = tripled(turned_modes[f][r.peer[0, 0, 4 * k + f]])
        image = jnp.dot(
            r.basis[:, f, :, 0:256].reshape(size // 4, 256),
            jnp.concatenate([start_here, -start_near[f]], axis=0),
            preferred_element_type=F32,
        ).reshape(4, 128, 128)
        spread_start = jnp.dot(
            r.basis[:, f, :, 256:384].reshape(size // 4, 128),
            start_here,
            preferred_element_type=F32,
        ).reshape(4, 128, 128)
        r.lam[f] = spread_start
        for k in range(4):
            r.z0[f, k] = r.load[f, k] - halo[0][f][r.peer[0, 0, 4 * k + f]] - image[k]

    out_lam = pltpu.make_async_copy(r.lam, r.lam_hbm, r.osem.at[0])
    out_lam.start()

    def joined(tile):
        parts = []
        for t in range(C):
            part = tile(t, 0)
            if t > 0:
                part = part - tile(t - 1, 2)
            if t < C - 1:
                part = part - tile(t + 1, 1)
            parts += [part, blank]
        return filled(jnp.concatenate(parts, axis=0))

    def load_term(t, kind):
        return r.rb0[t % 2, t // 2, MODES * kind : MODES * (kind + 1)]

    tile_lanes = lax.broadcasted_iota(jnp.int32, (MODES, 128), 1)

    def mode_term(t, kind):
        value = r.kb[t, 0:MODES]
        value = jnp.where((tile_lanes >= 32 * kind) & (tile_lanes < 32 * kind + 3 * PAD), value, 0.0)
        turn = (PAD * (t - 1) - 32 * kind) % 128
        return pltpu.roll(value, turn, 1) if turn else value

    cluster_wait(r.kb, 0)
    gfg = joined(mode_term)
    coarse_now = joined(load_term) - jnp.dot(gfg, start, precision=HIGHEST)
    first = solve(coarse_now)
    keep(1, first)
    weights = packed(near(1, 0))

    half_on = [jnp.where(has[f], 0.5, 1.0) for f in range(4)]

    def folded(value):
        return jnp.sum(value.reshape(-1, PAD, 128), axis=0)

    def column_sum(parts):
        return jnp.sum(parts, axis=0, keepdims=True)

    def spread(weights, f):
        return jnp.dot(
            r.basis[:, f, :, 256:384].reshape(size // 4, 128), weights, preferred_element_type=F32
        ).reshape(4, 128, 128)

    row_ids = lax.broadcasted_iota(jnp.int32, (3 * PAD, 128), 0)

    def with_rows(terms, scalars):
        for row, value in scalars:
            terms = jnp.where(row_ids == row, value, terms)
        return terms

    norm = jnp.zeros((PAD, 128), F32)
    for f in range(4):
        value = r.z0[f] - spread(weights, f)
        r.z0[f] = value
        r.rhs[:, f, :, 0:128] = value.astype(BF16)
        norm = norm + half_on[f] * folded(value * value)
    out_z0 = pltpu.make_async_copy(r.z0, r.z0_hbm, r.osem.at[1])
    out_z0.start()
    r.ra2[s] = with_rows(field_terms(r.d3, r.z0), [(6, column_sum(norm))])
    sub_start(r.ra2, 2)

    for f in range(4):
        r.im0[f] = jnp.dot(
            r.dual[:, f].reshape(size // 4, size),
            r.rhs[:, :, :, 0:128].reshape(size, 128),
            preferred_element_type=F32,
        ).reshape(4, 128, 128)

        @pl.when(has[f])
        def _():
            halo_copy(r.im0, 1, f).start()

    columns = filled(r.cinv[pl.ds(PAD * c, 3 * PAD), :]).T[:, 0 : 3 * PAD]
    own_inverse = r.cinv[pl.ds(PAD * (c + 1), PAD), :]
    r.rb2[core, z] = sub_total(r.ra2, 2)
    chips_start(r.rb2, 1)

    for f in range(4):

        @pl.when(has[f])
        def _():
            wait_bytes(halo[1][f], r.hrecv.at[1, f])

    square = jnp.zeros((PAD, 128), F32)
    cross = jnp.zeros((PAD, 128), F32)
    for f in range(4):
        for k in range(4):
            value = r.im0[f, k] - halo[1][f][r.peer[0, 0, 4 * k + f]]
            r.y[f, k] = value
            high, low = split(value)
            r.rhs[k, f, :, 0:128] = high
            r.rhs[k, f, :, 128:256] = low
            square = square + half_on[f] * folded(value * value)
            cross = cross + half_on[f] * folded(value * r.z0[f, k])
    r.ra3[s] = with_rows(
        field_terms(r.d3, r.y), [(6, column_sum(square)), (7, column_sum(cross))]
    )
    sub_start(r.ra3, 3)

    energy = jnp.zeros((PAD, 128), F32)
    for f in range(4):
        pair = jnp.dot(
            r.dual[:, f].reshape(size // 4, size),
            r.rhs[...].reshape(size, 256),
            preferred_element_type=F32,
        )
        part = (pair[:, :128] + pair[:, 128:]).reshape(4, 128, 128)
        energy = energy + folded(r.y[f] * part)
        if f == 1:
            chips_end(r.rb2, 1)
    r.sa[s] = column_sum(energy)
    sub_start(r.sa, 4)

    cores_end(r.rb2, 1)
    norm_now = r.rb2[0, 0, 6:7]
    for t in range(1, C):
        norm_now = norm_now + r.rb2[t % 2, t // 2, 6:7]
    parts = []
    for t in range(C):
        part = r.rb2[t % 2, t // 2, PAD : 2 * PAD]
        if t > 0:
            part = part + r.rb2[(t - 1) % 2, (t - 1) // 2, 2 * PAD : 3 * PAD]
        if t < C - 1:
            part = part + r.rb2[(t + 1) % 2, (t + 1) // 2, 0:PAD]
        parts.append(part)
    coarse_image = filled(jnp.concatenate(parts, axis=0))
    shift = solve(coarse_image)
    keep(2, shift)
    shift = filled(shift)
    near_shift = near(2, 0)

    total = sub_total(r.ra3, 3)
    answers = jnp.dot(columns, total, precision=HIGHEST)
    tile_rows = lax.broadcasted_iota(jnp.int32, (PAD, 128), 0)
    for t in range(C):
        tile = answers[PAD * t : PAD * (t + 1)]
        r.ub3[t] = jnp.where(tile_rows < 6, tile, total[0:PAD])
    r.rb3[c] = r.ub3[c]
    cluster_start(lambda there: r.ub3.at[there], r.rb3, 3)

    bent = jnp.dot(gfg, shift, precision=HIGHEST)
    overlap = column_sum(coarse_image * shift)
    bent_energy = column_sum(bent * shift)
    shift_energy = 2.0 * column_sum(near_shift * total)

    r.sb[c] = sub_total(r.sa, 4) - shift_energy
    cluster_start(lambda there: r.sb.at[c], r.sb, 4)

    bent_own = jnp.dot(own_inverse, bent, precision=HIGHEST)
    shift_own = near_shift[PAD : 2 * PAD]
    first_own = near(1, 0)[PAD : 2 * PAD]
    weights = packed(near_shift)
    for f in range(4):
        r.y[f] = r.y[f] - spread(weights, f)
    out_w = pltpu.make_async_copy(r.y, r.w_hbm, r.osem.at[2])
    out_w.start()

    total = cluster_total(r.rb3, 3)
    curvature_now = total[7:8]
    length = norm_now / curvature_now
    w_square = total[6:7] - overlap
    w_energy = cluster_total(r.sb, 4) + bent_energy
    norm_next = length * length * w_square - norm_now
    ratio = norm_next / norm_now
    z_energy = curvature_now - 2.0 * length * w_square + length * length * w_energy
    zd_energy = curvature_now - length * w_square
    curvature_next = z_energy + 2.0 * ratio * zd_energy + ratio * ratio * curvature_now
    step = norm_next / curvature_next
    last = (
        first_own
        - length * shift_own
        - step * ((1.0 + ratio) * shift_own - length * (total - bent_own))
    )
    r.last_out[0:PAD] = last
    r.last_out[PAD : PAD + 1] = length + step * (1.0 + ratio)
    r.last_out[PAD + 1 : PAD + 2] = step * length

    for k, buf in enumerate([r.ka, r.ra0, r.ra2, r.ra3, r.sa]):
        wait_bytes(buf.at[pl.ds(0, S - 1)], r.asend.at[k])
    wait_bytes(r.eb.at[pl.ds(0, C - 1)], r.esend)
    for k, buf in enumerate([r.rb0, r.rb2]):
        wait_bytes(buf.at[0, pl.ds(0, Z - 1)], r.zsend.at[k])
        wait_bytes(buf.at[0], r.ksend.at[k])
    for k, buf in ((0, r.kb), (3, r.rb3), (4, r.sb)):
        wait_bytes(buf.at[pl.ds(0, C - 1)], r.bsend.at[k])
    for f in range(4):

        @pl.when(has[f])
        def _():
            halo_copy(r.load, 0, f).wait_send()
            halo_copy(r.im0, 1, f).wait_send()
            modes_copy(f).wait_send()

    out_lam.wait()
    out_z0.wait()
    out_w.wait()


def finish(sign, last_hbm, lam_hbm, z0_hbm, w_hbm, out_hbm, amp_hbm, last, lam, z0, w, amp, sems):
    cp_last = pltpu.make_async_copy(last_hbm, last, sems.at[4, 0])
    cp_last.start()
    copies = [
        [
            pltpu.make_async_copy(src.at[f], dst.at[f], sems.at[f, i])
            for i, (src, dst) in enumerate(((lam_hbm, lam), (z0_hbm, z0), (w_hbm, w)))
        ]
        for f in range(4)
    ]
    for group in copies:
        for copy in group:
            copy.start()
    cp_last.wait()
    grow, back = last[PAD : PAD + 1], last[PAD + 1 : PAD + 2]
    amp[:, 0] = last[:MODES]
    results = [pltpu.make_async_copy(amp, amp_hbm, sems.at[4, 1])]
    results[0].start()
    for f in range(4):
        for copy in copies[f]:
            copy.wait()
        for k in range(4):
            turned = sign[0, 0, 4 * k + f].astype(F32)
            lam[f, k] = turned * (lam[f, k] + grow * z0[f, k] - back * w[f, k])
        for k in range(4):
            result = pltpu.make_async_copy(lam.at[f, k], out_hbm.at[k, f], sems.at[5 + f, k])
            result.start()
            results.append(result)
    for result in results:
        result.wait()


def per_device(C, S, dual_ops, local_load, rigid_modes, coarse_load, gluing_peer, gluing_sign):
    size = dual_ops.shape[-1]
    block = size // 16
    loads = local_load.shape[-1]
    hbm = pl.BlockSpec(memory_space=pltpu.HBM)
    dma = pltpu.SemaphoreType.DMA
    field = pltpu.VMEM((4, 4, block, loads), F32)

    def rows(*shape):
        return pltpu.VMEM((*shape, 128), F32)

    scratch = dict(
        peer=pltpu.SMEM((1, 1, 16), jnp.int32),
        dual=pltpu.VMEM((4, 4, block, size), BF16),
        load=field,
        modes=pltpu.VMEM((MODES, 16, block), F32),
        cload=pltpu.VMEM((MODES, 1, loads), F32),
        lam=field,
        z0=field,
        y=field,
        im0=field,
        rhs=pltpu.VMEM((4, 4, block, 2 * loads), BF16),
        basis=pltpu.VMEM((4, 4, block, 384), BF16),
        t3=pltpu.VMEM((6 * PAD, size), BF16),
        d3=pltpu.VMEM((6 * PAD, size), BF16),
        cinv=rows(PAD * (C + 2)),
        coef=rows(3, PAD * (C + 4)),
        msg=rows(4, block),
        ka=rows(S, PAD),
        kb=rows(C, PAD),
        eb=rows(C, PAD),
        ra0=rows(S, 4 * MODES),
        rb0=rows(2, C // 2, 4 * MODES),
        ra2=rows(S, 3 * PAD),
        rb2=rows(2, C // 2, 3 * PAD),
        ra3=rows(S, 3 * PAD),
        ub3=rows(C, PAD),
        rb3=rows(C, PAD),
        sa=rows(S, 1),
        sb=rows(C, 1),
        lsem=dma((8,)),
        dsem=dma,
        osem=dma((3,)),
        hsend=dma((2, 4)),
        hrecv=dma((2, 4)),
        gsend=dma((4,)),
        grecv=dma((4,)),
        asend=dma((5,)),
        arecv=dma((5,)),
        bsend=dma((5,)),
        brecv=dma((5,)),
        zsend=dma((2,)),
        zrecv=dma((2, C // 2)),
        ksend=dma((2,)),
        krecv=dma((2,)),
        esend=dma,
        erecv=dma,
    )
    for f in range(4):
        scratch["h0%d" % f] = rows(4, block)
        scratch["h1%d" % f] = rows(4, block)
        scratch["a%d" % f] = rows(block)
        scratch["r%d" % f] = rows(4, block)
    whole = jax.ShapeDtypeStruct((4, 4, block, loads), F32)
    lam, z0, w, last = pl.pallas_call(
        functools.partial(kernel, C, S),
        out_shape=(whole, whole, whole, jax.ShapeDtypeStruct((2 * PAD, loads), F32)),
        in_specs=[hbm] * 5,
        out_specs=(hbm, hbm, hbm, pl.BlockSpec(memory_space=pltpu.VMEM)),
        scratch_shapes=[scratch[name] for name in NAMES[9:]],
        compiler_params=pltpu.CompilerParams(
            collective_id=0, has_side_effects=True, vmem_limit_bytes=56 * 1024 * 1024
        ),
    )(
        gluing_peer,
        dual_ops.reshape(4, 4, block, size),
        local_load.reshape(4, 4, block, loads),
        rigid_modes.reshape(MODES, 16, block),
        coarse_load.reshape(MODES, 1, loads),
    )
    multipliers, amplitudes = pl.pallas_call(
        finish,
        out_shape=(whole, jax.ShapeDtypeStruct((MODES, 1, loads), F32)),
        in_specs=[pl.BlockSpec(memory_space=pltpu.SMEM)] + [hbm] * 4,
        out_specs=(hbm, hbm),
        scratch_shapes=[
            rows(2 * PAD),
            field,
            field,
            field,
            pltpu.VMEM((MODES, 1, loads), F32),
            dma((9, 4)),
        ],
    )(gluing_sign, last, lam, z0, w)
    return multipliers.reshape(1, 1, size, loads), amplitudes.reshape(1, MODES, loads)


def solution(mesh):
    return jax.shard_map(
        functools.partial(per_device, mesh.shape["cluster"], mesh.shape["sub"]),
        mesh=mesh,
        in_specs=(
            P("cluster", "sub", None, None),
            P("cluster", "sub", None, None),
            P("cluster", "sub", None, None),
            P("cluster", None, None),
            P("cluster", "sub", None),
            P("cluster", "sub", None),
        ),
        out_specs=(P("cluster", "sub", None, None), P("cluster", None, None)),
        check_vma=False,
    )
```
